32 devices in a mesh: groups: 2 (over y), inst: 4 (over z), tp: 2 (over x), rep: 2 (over core).
Axes of the slice: x: 2, y: 2, z: 4, core: 2. Of those that a mesh axis runs over, the one named last changes fastest.
Arguments:
- queries: bfloat16 [8, 32, 8192], P(('groups', 'rep'), 'inst', 'tp'), parts along dimension 0, may hold values from -8 to 8, as said below
- tool_key_value: bfloat16 [8, 32, 2048], P(('groups', 'rep'), 'inst', 'tp'), parts along dimension 0, may hold values from -8 to 8, as said below
- cache: bfloat16 [8, 3072, 2048], P(('groups', 'rep'), 'inst', 'tp'), parts along dimension 0, may hold values from -6 to 6
- placed: int32 [8, 4], P(('groups', 'rep'), 'inst'), parts along dimension 0, may hold values 0 or 1
- blocks: int32 [8, 4], P(('groups', 'rep'), 'inst'), parts along dimension 0, may hold values from 1 to 6
- span_len: int32 [8], P(('groups', 'rep')), parts along dimension 0, may hold values from 8 to 32
- owner: int32 [8], P(('groups', 'rep')), parts along dimension 0, may hold values from 0 to 3, as said below
Outputs:
- attended: bfloat16 [8, 32, 8192], P(('groups', 'rep'), 'inst', 'tp'), parts along dimension 0
- owned: bfloat16 [8, 2, 32, 2048], P(('groups', 'inst'), 'rep', None, 'tp'), parts along dimension 0
The draws below stay inside these ranges and needn't reach their ends.
There are 2 independent parts, one for each index of `groups`. The reference program is written for one: setup_inputs(seed, part) draws one part's arguments, and reference() takes and returns one part's arrays. A program takes and returns all parts, laid end to end along the dimension named above; each array names one. Nothing has to cross between parts.
Inputs may be any that keep to these rules, and one draw needn't show every extreme that they name: real-valued rotated queries. `tool_key_value`: real-valued rotated keys and values. `owner`: the 2 forks of one index of rep have different owners.
All inputs are finite; a program needn't handle non-finite values. No bound on the sum of `placed` on one device may be relied on, other than what follows from the above.
Results may differ from the reference program's by a relative error of at most 0.0022.
Values may be sent and summed in bfloat16 or wider, within the bound.
A program may use at most 128 MiB of HBM per device.

```python
import math
import jax
import jax.numpy as jnp
from jax import lax

QUERY_HEADS = 64
KEY_HEADS = 8
HEAD_DIM = 128
BLOCK = 128
CAPB = 6
C_DEV = 8
F_REP = 2
FORK_TOTAL = 4
TOOL_SPAN = 32
CAP = 768
CACHE_SLOTS = 3072
N_INST = 4
N_REP = 2


def draw_queries(key, part):
    own_key = jax.random.fold_in(key, 11)
    complete_shape = (FORK_TOTAL, TOOL_SPAN, QUERY_HEADS, HEAD_DIM)
    base_offset = jnp.clip(2.5 * jax.random.normal(own_key, complete_shape, jnp.float32), -8.0, 8.0)
    return base_offset.reshape(FORK_TOTAL, TOOL_SPAN, QUERY_HEADS * HEAD_DIM).astype(jnp.bfloat16)


def draw_tool_key_value(key, part):
    own_key = jax.random.fold_in(key, 13)
    complete_shape = (FORK_TOTAL, TOOL_SPAN, KEY_HEADS, 2, HEAD_DIM)
    base_offset = jnp.clip(jax.random.normal(own_key, complete_shape, jnp.float32), -6.0, 6.0)
    return base_offset.reshape(FORK_TOTAL, TOOL_SPAN, KEY_HEADS * 2 * HEAD_DIM).astype(jnp.bfloat16)


def draw_owner(key, part):
    groups_list = []
    for replica in range(FORK_TOTAL // F_REP):
        order = jax.random.permutation(jax.random.fold_in(key, 31 + replica), N_INST)
        groups_list.append(order[:F_REP].astype(jnp.int32))
    return jnp.concatenate(groups_list).astype(jnp.int32)


def with_ends(result, rng, smallest, largest):
    dims = result.shape
    index_at = [jax.random.randint(jax.random.fold_in(rng, axis), (), 0, dims[axis]) for axis in range(len(dims))]
    result = result.at[tuple(index_at)].set(smallest)
    longest = dims.index(max(dims))
    index_at[longest] = (index_at[longest] + 1) % dims[longest]
    return result.at[tuple(index_at)].set(largest)


def shard_levels(stream_key, extent, cuts, low, top_value):
    gain = 1.0
    for position, shards_of in cuts:
        heights = jax.random.uniform(jax.random.fold_in(jax.random.fold_in(stream_key, 6), position), (shards_of,), jnp.float32, low / len(cuts), top_value / len(cuts))
        gain = gain * jnp.repeat(jnp.exp(heights), extent[position] // shards_of).reshape((-1,) + (1,) * (len(extent) - 1 - position))
    return gain


def gaussian(key, dims, width, reach, cuts=(), kind=jnp.bfloat16):
    loudness = shard_levels(key, dims, cuts, -0.22, 0.18) if cuts else 1.0
    entries = jax.random.normal(key, dims, jnp.float32) * width * loudness
    return jnp.minimum(jnp.maximum(entries, -reach), reach).astype(kind)


def setup_inputs(seed: int = 0, part: int = 0) -> dict:
    seeds = jax.random.split(jax.random.key(seed), 8)
    part_keys = jax.random.split(jax.random.fold_in(seeds[7], part), 8)
    return {
        "queries": draw_queries(jax.random.fold_in(jax.random.fold_in(seeds[7], part), 71), part),
        "tool_key_value": draw_tool_key_value(jax.random.fold_in(jax.random.fold_in(seeds[7], part), 71), part),
        "cache": gaussian(part_keys[2], (FORK_TOTAL, CACHE_SLOTS, KEY_HEADS * 2 * HEAD_DIM), 1.0, 6.0, ((0, 2), (1, 4), (2, 2))),
        "placed": with_ends((jax.random.randint(part_keys[3], (FORK_TOTAL, N_INST), 0, 4) < 3).astype(jnp.int32), jax.random.fold_in(part_keys[3], 1), 0, 1),
        "blocks": with_ends(jax.random.randint(part_keys[4], (FORK_TOTAL, N_INST), 1, CAPB + 1), jax.random.fold_in(part_keys[4], 1), 1, CAPB).astype(jnp.int32),
        "span_len": with_ends(jax.random.randint(part_keys[5], (FORK_TOTAL,), TOOL_SPAN // 4, TOOL_SPAN + 1), jax.random.fold_in(part_keys[5], 1), TOOL_SPAN // 4, TOOL_SPAN).astype(jnp.int32),
        "owner": draw_owner(jax.random.fold_in(jax.random.fold_in(seeds[7], part), 71), part),
    }


def reference(queries, tool_key_value, cache, placed, blocks, span_len, owner):
    query_group_size = QUERY_HEADS // KEY_HEADS
    scaling = 1.0 / math.sqrt(HEAD_DIM)
    query_matrix = queries.reshape(FORK_TOTAL, TOOL_SPAN, KEY_HEADS, query_group_size, HEAD_DIM)
    fresh_kv_rows = tool_key_value.reshape(FORK_TOTAL, TOOL_SPAN, KEY_HEADS, 2, HEAD_DIM)
    stored_cache_rows = cache.reshape(FORK_TOTAL, CACHE_SLOTS, KEY_HEADS, 2, HEAD_DIM)
    within = jnp.arange(CAP, dtype=jnp.int32)
    tokens_all = jnp.arange(TOOL_SPAN, dtype=jnp.int32)
    causal = (tokens_all[None, :] <= tokens_all[:, None]).reshape(TOOL_SPAN, N_INST, C_DEV)

    def one_fork(fork_id):
        live_len = placed[fork_id] * blocks[fork_id] * BLOCK
        live = within[None, :] < live_len[:, None]
        mask_all = jnp.concatenate([jnp.broadcast_to(live[None], (TOOL_SPAN, N_INST, CAP)), causal], axis=2)
        mask_all = mask_all[:, None, :, :]

        def single_head(head_id):
            query = query_matrix[fork_id, :, head_id].astype(jnp.float32)
            key_old = stored_cache_rows[fork_id, :, head_id, 0].astype(jnp.float32).reshape(N_INST, CAP, HEAD_DIM)
            value_old = stored_cache_rows[fork_id, :, head_id, 1].astype(jnp.float32).reshape(N_INST, CAP, HEAD_DIM)
            key_new = fresh_kv_rows[fork_id, :, head_id, 0].astype(jnp.float32).reshape(N_INST, C_DEV, HEAD_DIM)
            value_new = fresh_kv_rows[fork_id, :, head_id, 1].astype(jnp.float32).reshape(N_INST, C_DEV, HEAD_DIM)
            key_all = jnp.concatenate([key_old, key_new], axis=1)
            value_all = jnp.concatenate([value_old, value_new], axis=1)
            score = jnp.einsum('tgd,ipd->tgip', query, key_all) * scaling
            part_max = lax.optimization_barrier(jnp.max(jnp.where(mask_all, score, -jnp.inf), axis=-1))
            safe_max = jnp.where(part_max > -jnp.inf, part_max, 0.0)
            weight = jnp.where(mask_all, jnp.exp(score - safe_max[..., None]), 0.0)
            part_total = lax.optimization_barrier(jnp.sum(weight, axis=-1))
            rounded = lax.optimization_barrier(weight.astype(jnp.bfloat16)).astype(jnp.float32)
            part_numer = jnp.einsum('tgip,ipd->tgid', rounded, value_all)
            highest = lax.optimization_barrier(jnp.max(part_max, axis=-1))
            factor = jnp.where(part_max > -jnp.inf, jnp.exp(safe_max - highest[..., None]), 0.0)
            total = lax.optimization_barrier(jnp.sum(factor * part_total, axis=-1))
            numer = lax.optimization_barrier(jnp.sum(factor[..., None] * part_numer, axis=-2))
            return numer / total[..., None]
        return lax.map(single_head, jnp.arange(KEY_HEADS, dtype=jnp.int32))
    heads_out = lax.map(one_fork, jnp.arange(FORK_TOTAL, dtype=jnp.int32))
    attended = jnp.transpose(heads_out, (0, 2, 1, 3, 4)).reshape(FORK_TOTAL, TOOL_SPAN, QUERY_HEADS * HEAD_DIM)
    valid = tokens_all[None, :] < span_len[:, None]
    attended = jnp.where(valid[:, :, None], attended, 0.0).astype(jnp.bfloat16)
    kept = jnp.where(valid[:, :, None], tool_key_value, jnp.zeros((), tool_key_value.dtype)).astype(jnp.float32)
    rep_of = jnp.arange(FORK_TOTAL, dtype=jnp.int32) // F_REP
    chosen = (owner[None, None, :] == jnp.arange(N_INST, dtype=jnp.int32)[:, None, None]) & (rep_of[None, None, :] == jnp.arange(N_REP, dtype=jnp.int32)[None, :, None])
    owned = jnp.einsum('irf,ftk->irtk', chosen.astype(jnp.float32), kept).astype(jnp.bfloat16)
    return (attended, owned)
```

```python
import functools
import math

import jax
import jax.numpy as jnp
from jax import lax
from jax.experimental import pallas as pl
from jax.experimental.pallas import tpu as pltpu
from jax.sharding import PartitionSpec as P

HEAD_DIM = 128
BLOCK = 128
FRESH_ROWS = 16
CHUNKS = 4
STEPS = 32000.0
LOG2E = 1.4426950408889634
HIDDEN = -1e30
FLOOR = -1e5
MESH = pl.DeviceIdType.MESH
NT = (((1,), (1,)), ((), ()))
TN = (((0,), (0,)), ((), ()))


def kernel(
    n, q_ref, kv_ref, cache_ref, placed_ref, blocks_ref, span_ref, owner_ref,
    att_ref, owned_ref,
    cbuf, vt, kf, vf, qbuf, pn, ps, ci, cis, co, cos, po, pi,
    cache_sem, q_send, q_recv, c_send, s_send, c_recv, s_recv, o_send, o_recv,
):
    forks, tokens, width = q_ref.shape
    width_kv = kv_ref.shape[2]
    kv_heads = width_kv // (2 * HEAD_DIM)
    group = width // (kv_heads * HEAD_DIM)
    rows = group * tokens
    lanes = 2 * rows
    pairs = forks * kv_heads // 2
    slots = cache_ref.shape[1]
    per = pairs // CHUNKS
    factor = LOG2E / math.sqrt(HEAD_DIM)
    me = lax.axis_index("inst")

    fetches = [
        pltpu.make_async_copy(cache_ref.at[f], cbuf.at[f], cache_sem.at[f])
        for f in range(forks)
    ]
    for fetch in fetches:
        fetch.start()

    barrier = pltpu.get_barrier_semaphore()
    for k in range(1, n):
        pl.semaphore_signal(
            barrier, inc=1, device_id={"inst": lax.rem(me + k, n)}, device_id_type=MESH
        )

    def members(p):
        return [(u // kv_heads, u % kv_heads) for u in (2 * p, 2 * p + 1)]

    for p in range(pairs):
        parts = []
        for f, j in members(p):
            for g in range(group):
                at = (j * group + g) * HEAD_DIM
                parts.append(q_ref[f, :, at : at + HEAD_DIM].astype(jnp.float32))
        qbuf[me, p] = jnp.concatenate(parts, axis=0).astype(jnp.bfloat16)

    pl.semaphore_wait(barrier, n - 1)

    def q_copy(origin, c, side):
        part = qbuf.at[origin, pl.ds(c * per, per)]
        return pltpu.make_async_remote_copy(
            src_ref=part, dst_ref=part,
            send_sem=q_send.at[side, origin, c], recv_sem=q_recv.at[origin, c],
            device_id={"inst": me + 1 if side == 0 else me - 1}, device_id_type=MESH,
        )

    for c in range(CHUNKS):
        for side in range(2):
            @pl.when(me + 1 < n if side == 0 else me > 0)
            def _():
                q_copy(me, c, side).start()

    for i in range(n):
        chosen = None
        for f in range(forks):
            tile = kv_ref[f].astype(jnp.float32)
            token = me * tokens + lax.broadcasted_iota(jnp.int32, tile.shape, 0)
            keep = (token < span_ref[f]) & (jnp.broadcast_to(owner_ref[f], tile.shape) == i)
            tile = jnp.where(keep, tile, 0.0)
            chosen = tile if chosen is None else chosen + tile
        po[i] = jnp.concatenate(
            [chosen[:, a : a + HEAD_DIM] for a in range(0, width_kv, HEAD_DIM)], axis=0
        ).astype(jnp.bfloat16)
    pi[me] = po[me]

    def parcel(k):
        target = lax.rem(me + k, n)
        return pltpu.make_async_remote_copy(
            src_ref=po.at[target], dst_ref=pi.at[me],
            send_sem=o_send.at[target], recv_sem=o_recv.at[me],
            device_id={"inst": target}, device_id_type=MESH,
        )

    for k in range(1, n):
        parcel(k).start()

    for p in range(pairs):
        for ref, shift in ((kf, 0), (vf, HEAD_DIM)):
            both = [
                kv_ref[f, :, 2 * j * HEAD_DIM + shift : 2 * j * HEAD_DIM + shift + HEAD_DIM]
                for f, j in members(p)
            ]
            tile = jnp.concatenate(both, axis=1).astype(jnp.float32)
            pad = jnp.zeros((FRESH_ROWS - tokens, 2 * HEAD_DIM), jnp.float32)
            ref[p] = jnp.concatenate([tile, pad], axis=0).astype(jnp.bfloat16)

    for fetch in fetches:
        fetch.wait()
    for p in range(pairs):
        for h, (f, j) in enumerate(members(p)):
            at = (2 * j + 1) * HEAD_DIM
            vt[p, h * HEAD_DIM : (h + 1) * HEAD_DIM, :] = cbuf[f, :, at : at + HEAD_DIM].T

    lane = lax.broadcasted_iota(jnp.int32, (1, lanes), 1)
    lane_token = lax.rem(lane, tokens)
    first = lane < rows

    def by_lane(p, value):
        (f0, _), (f1, _) = members(p)
        return jnp.where(first, value(f0), value(f1))

    def attend(origin, p):
        tile = qbuf[origin, p]
        blank = jnp.zeros((rows, HEAD_DIM), jnp.bfloat16)
        spread = jnp.concatenate(
            [
                jnp.concatenate([tile[:rows], blank], axis=1),
                jnp.concatenate([blank, tile[rows:]], axis=1),
            ],
            axis=0,
        )
        keys = jnp.concatenate(
            [cbuf[f, :, 2 * j * HEAD_DIM : (2 * j + 1) * HEAD_DIM] for f, j in members(p)], axis=1
        )
        score = lax.dot_general(keys, spread, NT, preferred_element_type=jnp.float32) * factor
        score_new = lax.dot_general(kf[p], spread, NT, preferred_element_type=jnp.float32) * factor
        live = by_lane(p, lambda f: placed_ref[f, 0] * blocks_ref[f, 0] * BLOCK)
        slot = lax.broadcasted_iota(jnp.int32, (slots, lanes), 0)
        score = jnp.where(slot < live, score, HIDDEN)
        row = lax.broadcasted_iota(jnp.int32, (FRESH_ROWS, lanes), 0)
        counted = (row < tokens) & (me * tokens + row <= origin * tokens + lane_token)
        score_new = jnp.where(counted, score_new, HIDDEN)
        top = jnp.maximum(
            jnp.max(score, axis=0, keepdims=True), jnp.max(score_new, axis=0, keepdims=True)
        )
        top = jnp.maximum(top, FLOOR)
        weight = jnp.exp2(score - top)
        weight_new = jnp.exp2(score_new - top)
        total = jnp.sum(weight, axis=0, keepdims=True) + jnp.sum(weight_new, axis=0, keepdims=True)
        both = jnp.dot(vt[p], weight.astype(jnp.bfloat16), preferred_element_type=jnp.float32)
        both = both + lax.dot_general(
            vf[p], weight_new.astype(jnp.bfloat16), TN, preferred_element_type=jnp.float32
        )
        numer = jnp.where(first, both[:HEAD_DIM], both[HEAD_DIM:])
        pn[origin, p] = numer
        ps[origin, p, 0:1] = top
        ps[origin, p, 1:2] = total

    def kept(d, p):
        return pn[d, p], ps[d, p, 0:1], ps[d, p, 1:2]

    def arrived(slot, p):
        numer = ci[slot, p].astype(jnp.int32).astype(jnp.float32) * cis[slot, p, 2:3]
        return numer, cis[slot, p, 0:1], cis[slot, p, 1:2]

    def merge(one, two):
        top = jnp.maximum(one[1], two[1])
        a = jnp.exp2(one[1] - top)
        b = jnp.exp2(two[1] - top)
        return a * one[0] + b * two[0], top, a * one[2] + b * two[2]

    def pack(d, p, part):
        numer, top, total = part
        reach = jnp.maximum(jnp.max(jnp.abs(numer), axis=0, keepdims=True), 1e-30)
        co[d, p] = jnp.round(numer * (STEPS / reach)).astype(jnp.int32).astype(jnp.int16)
        row = lax.broadcasted_iota(jnp.int32, (8, lanes), 0)
        cos[d, p] = jnp.where(row == 0, top, jnp.where(row == 1, total, reach * (1.0 / STEPS)))

    def chain_copies(d, c, side):
        target = me + 1 if side == 0 else me - 1
        slot = d if side == 0 else jnp.where(d == target, n, d)
        part = pl.ds(c * per, per)
        where = dict(device_id={"inst": target}, device_id_type=MESH)
        return (
            pltpu.make_async_remote_copy(
                src_ref=co.at[d, part], dst_ref=ci.at[slot, part],
                send_sem=c_send.at[d, c], recv_sem=c_recv.at[slot, c], **where
            ),
            pltpu.make_async_remote_copy(
                src_ref=cos.at[d, part], dst_ref=cis.at[slot, part],
                send_sem=s_send.at[d, c], recv_sem=s_recv.at[slot, c], **where
            ),
        )

    def chain_arrival(slot, c):
        part = pl.ds(c * per, per)
        pltpu.make_async_copy(ci.at[slot, part], ci.at[slot, part], c_recv.at[slot, c]).wait()
        pltpu.make_async_copy(cis.at[slot, part], cis.at[slot, part], s_recv.at[slot, c]).wait()

    for p in range(pairs):
        attend(me, p)

    def advance(t, carry):
        for c in range(CHUNKS):
            for side in range(2):
                origin = me - t if side == 0 else me + t
                there = (t < n) & (origin >= 0 if side == 0 else origin < n)

                @pl.when(there)
                def _():
                    q_copy(origin, c, side).wait_recv()

                    @pl.when(me + 1 < n if side == 0 else me > 0)
                    def _():
                        q_copy(origin, c, side).start()

                    for p in range(c * per, (c + 1) * per):
                        attend(origin, p)

            for side in range(2):
                place = me if side == 0 else n - 1 - me
                far = t - place
                d = far if side == 0 else n - 1 - far

                @pl.when((far > place) & (far < n))
                def _():
                    @pl.when(place == 0)
                    def _():
                        for p in range(c * per, (c + 1) * per):
                            pack(d, p, kept(d, p))

                    @pl.when(place > 0)
                    def _():
                        chain_arrival(d, c)
                        for p in range(c * per, (c + 1) * per):
                            pack(d, p, merge(kept(d, p), arrived(d, p)))

                    for copy in chain_copies(d, c, side):
                        copy.start()
        return carry

    lax.fori_loop(1, 2 * n - 1, advance, 0)

    for k in range(1, n):
        source = lax.rem(me + n - k, n)
        pltpu.make_async_copy(pi.at[source], pi.at[source], o_recv.at[source]).wait()
    gathered = [pi[i].astype(jnp.float32) for i in range(n)]
    for a in range(width_kv // HEAD_DIM):
        column = jnp.concatenate([x[a * tokens : (a + 1) * tokens] for x in gathered], axis=0)
        owned_ref[0, 0, :, a * HEAD_DIM : (a + 1) * HEAD_DIM] = column.astype(jnp.bfloat16)

    for c in range(CHUNKS):
        for slot, there in ((me, me > 0), (n, me + 1 < n)):
            @pl.when(there)
            def _():
                chain_arrival(slot, c)
                for p in range(c * per, (c + 1) * per):
                    numer, top, total = merge(kept(me, p), arrived(slot, p))
                    pn[me, p] = numer
                    ps[me, p, 0:1] = top
                    ps[me, p, 1:2] = total

        for p in range(c * per, (c + 1) * per):
            numer, _, total = kept(me, p)
            span = by_lane(p, lambda f: span_ref[f])
            result = jnp.where(me * tokens + lane_token < span, numer / total, 0.0).T
            for h, (f, j) in enumerate(members(p)):
                for g in range(group):
                    at = (j * group + g) * HEAD_DIM
                    start = h * rows + g * tokens
                    att_ref[f, :, at : at + HEAD_DIM] = result[start : start + tokens].astype(
                        jnp.bfloat16
                    )

    for k in range(1, n):
        parcel(k).wait_send()
    for c in range(CHUNKS):
        for side in range(2):
            @pl.when(me + 1 < n if side == 0 else me > 0)
            def _():
                q_copy(me, c, side).wait_send()

    def drain(t, carry):
        for c in range(CHUNKS):
            for side in range(2):
                origin = me - t if side == 0 else me + t
                onward = me + 1 < n if side == 0 else me > 0

                @pl.when((origin >= 0 if side == 0 else origin < n) & onward)
                def _():
                    q_copy(origin, c, side).wait_send()

                d = me + t if side == 0 else me - t

                @pl.when(d < n if side == 0 else d >= 0)
                def _():
                    for copy in chain_copies(d, c, side):
                        copy.wait_send()
        return carry

    lax.fori_loop(1, n, drain, 0)


def body(queries, tool_key_value, cache, placed, blocks, span_len, owner):
    n = lax.axis_size("inst")
    forks, tokens, width = queries.shape
    width_kv = tool_key_value.shape[2]
    slots = cache.shape[1]
    kv_heads = width_kv // (2 * HEAD_DIM)
    group = width // (kv_heads * HEAD_DIM)
    pairs = forks * kv_heads // 2
    lanes = 2 * group * tokens
    parcel = (n, tokens * width_kv // HEAD_DIM, HEAD_DIM)
    bf16, f32, i16 = jnp.bfloat16, jnp.float32, jnp.int16
    vmem, smem = pltpu.VMEM, pltpu.SMEM
    dma = pltpu.SemaphoreType.DMA
    work = n * pairs * slots * lanes
    return pl.pallas_call(
        functools.partial(kernel, n),
        out_shape=(
            jax.ShapeDtypeStruct(queries.shape, bf16),
            jax.ShapeDtypeStruct((1, 1, n * tokens, width_kv), bf16),
        ),
        in_specs=[
            pl.BlockSpec(memory_space=vmem),
            pl.BlockSpec(memory_space=vmem),
            pl.BlockSpec(memory_space=pl.ANY),
        ]
        + [pl.BlockSpec(memory_space=smem)] * 4,
        out_specs=(pl.BlockSpec(memory_space=vmem), pl.BlockSpec(memory_space=vmem)),
        scratch_shapes=[
            vmem(cache.shape, bf16),
            vmem((pairs, 2 * HEAD_DIM, slots), bf16),
            vmem((pairs, FRESH_ROWS, 2 * HEAD_DIM), bf16),
            vmem((pairs, FRESH_ROWS, 2 * HEAD_DIM), bf16),
            vmem((n, pairs, lanes, HEAD_DIM), bf16),
            vmem((n, pairs, HEAD_DIM, lanes), f32),
            vmem((n, pairs, 8, lanes), f32),
            vmem((n + 1, pairs, HEAD_DIM, lanes), i16),
            vmem((n + 1, pairs, 8, lanes), f32),
            vmem((n, pairs, HEAD_DIM, lanes), i16),
            vmem((n, pairs, 8, lanes), f32),
            vmem(parcel, bf16),
            vmem(parcel, bf16),
            dma((forks,)),
            dma((2, n, CHUNKS)),
            dma((n, CHUNKS)),
            dma((n, CHUNKS)),
            dma((n, CHUNKS)),
            dma((n + 1, CHUNKS)),
            dma((n + 1, CHUNKS)),
            dma((n,)),
            dma((n,)),
        ],
        compiler_params=pltpu.CompilerParams(
            collective_id=0, has_side_effects=True, vmem_limit_bytes=48 * 1024 * 1024
        ),
        cost_estimate=pl.CostEstimate(
            flops=work * 8 * HEAD_DIM, bytes_accessed=2 * cache.size, transcendentals=work
        ),
    )(queries, tool_key_value, cache, placed, blocks, span_len, owner)


def solution(mesh):
    return jax.shard_map(
        body,
        mesh=mesh,
        in_specs=(
            P(("groups", "rep"), "inst", "tp"),
            P(("groups", "rep"), "inst", "tp"),
            P(("groups", "rep"), "inst", "tp"),
            P(("groups", "rep"), "inst"),
            P(("groups", "rep"), "inst"),
            P(("groups", "rep")),
            P(("groups", "rep")),
        ),
        out_specs=(P(("groups", "rep"), "inst", "tp"), P(("groups", "inst"), "rep", None, "tp")),
        check_vma=False,
    )
```

```python
import functools
import math

import jax
import jax.numpy as jnp
from jax import lax
from jax.experimental import pallas as pl
from jax.experimental.pallas import tpu as pltpu
from jax.sharding import PartitionSpec as P

HEAD_DIM = 128
BLOCK = 128
FRESH_ROWS = 16
CHUNKS = 4
STEPS = 32000.0
LOG2E = 1.4426950408889634
HIDDEN = -1e30
FLOOR = -1e5
MESH = pl.DeviceIdType.MESH
NT = (((1,), (1,)), ((), ()))
TN = (((0,), (0,)), ((), ()))


def kernel(
    n, q_hbm, kv_hbm, cache_ref, placed_hbm, blocks_hbm, span_hbm, owner_hbm,
    att_hbm, owned_hbm,
    att_ref, owned_ref, output_sem,
    q_ref, kv_ref, placed_ref, blocks_ref, span_ref, owner_ref, input_sem,
    cbuf, vt, kf, vf, qbuf, pn, ps, ci, cis, co, cos, po, pi,
    cache_sem, q_send, q_recv, c_send, s_send, c_recv, s_recv, o_send, o_recv,
):
    forks, tokens, width = q_ref.shape
    width_kv = kv_ref.shape[2]
    kv_heads = width_kv // (2 * HEAD_DIM)
    group = width // (kv_heads * HEAD_DIM)
    rows = group * tokens
    lanes = 2 * rows
    pairs = forks * kv_heads // 2
    slots = cache_ref.shape[1]
    per = pairs // CHUNKS
    factor = LOG2E / math.sqrt(HEAD_DIM)
    me = lax.axis_index("inst")

    inputs = [
        pltpu.make_async_copy(source, target, input_sem.at[k])
        for k, (source, target) in enumerate(
            (
                (q_hbm, q_ref), (kv_hbm, kv_ref), (placed_hbm, placed_ref),
                (blocks_hbm, blocks_ref), (span_hbm, span_ref), (owner_hbm, owner_ref),
            )
        )
    ]
    for fetch in inputs:
        fetch.start()
    fetches = [
        pltpu.make_async_copy(cache_ref.at[f], cbuf.at[f], cache_sem.at[f])
        for f in range(forks)
    ]
    for fetch in fetches:
        fetch.start()

    barrier = pltpu.get_barrier_semaphore()
    for k in range(1, n):
        pl.semaphore_signal(
            barrier, inc=1, device_id={"inst": lax.rem(me + k, n)}, device_id_type=MESH
        )

    def members(p):
        return [(u // kv_heads, u % kv_heads) for u in (2 * p, 2 * p + 1)]

    inputs[0].wait()
    for p in range(pairs):
        parts = []
        for f, j in members(p):
            for g in range(group):
                at = (j * group + g) * HEAD_DIM
                parts.append(q_ref[f, :, at : at + HEAD_DIM].astype(jnp.float32))
        qbuf[me, p] = jnp.concatenate(parts, axis=0).astype(jnp.bfloat16)

    pl.semaphore_wait(barrier, n - 1)

    def q_copy(origin, c, side):
        part = qbuf.at[origin, pl.ds(c * per, per)]
        return pltpu.make_async_remote_copy(
            src_ref=part, dst_ref=part,
            send_sem=q_send.at[side, origin, c], recv_sem=q_recv.at[origin, c],
            device_id={"inst": me + 1 if side == 0 else me - 1}, device_id_type=MESH,
        )

    for c in range(CHUNKS):
        for side in range(2):
            @pl.when(me + 1 < n if side == 0 else me > 0)
            def _():
                q_copy(me, c, side).start()

    for fetch in inputs[1:]:
        fetch.wait()
    for i in range(n):
        chosen = None
        for f in range(forks):
            tile = kv_ref[f].astype(jnp.float32)
            token = me * tokens + lax.broadcasted_iota(jnp.int32, tile.shape, 0)
            keep = (token < span_ref[f]) & (jnp.broadcast_to(owner_ref[f], tile.shape) == i)
            tile = jnp.where(keep, tile, 0.0)
            chosen = tile if chosen is None else chosen + tile
        po[i] = jnp.concatenate(
            [chosen[:, a : a + HEAD_DIM] for a in range(0, width_kv, HEAD_DIM)], axis=0
        ).astype(jnp.bfloat16)
    pi[me] = po[me]

    def parcel(k):
        target = lax.rem(me + k, n)
        return pltpu.make_async_remote_copy(
            src_ref=po.at[target], dst_ref=pi.at[me],
            send_sem=o_send.at[target], recv_sem=o_recv.at[me],
            device_id={"inst": target}, device_id_type=MESH,
        )

    for p in range(pairs):
        for ref, shift in ((kf, 0), (vf, HEAD_DIM)):
            both = [
                kv_ref[f, :, 2 * j * HEAD_DIM + shift : 2 * j * HEAD_DIM + shift + HEAD_DIM]
                for f, j in members(p)
            ]
            tile = jnp.concatenate(both, axis=1).astype(jnp.float32)
            pad = jnp.zeros((FRESH_ROWS - tokens, 2 * HEAD_DIM), jnp.float32)
            ref[p] = jnp.concatenate([tile, pad], axis=0).astype(jnp.bfloat16)

    for fetch in fetches:
        fetch.wait()
    for p in range(pairs):
        for h, (f, j) in enumerate(members(p)):
            at = (2 * j + 1) * HEAD_DIM
            vt[p, h * HEAD_DIM : (h + 1) * HEAD_DIM, :] = cbuf[f, :, at : at + HEAD_DIM].T

    lane = lax.broadcasted_iota(jnp.int32, (1, lanes), 1)
    lane_token = lax.rem(lane, tokens)
    first = lane < rows

    def by_lane(p, value):
        (f0, _), (f1, _) = members(p)
        return jnp.where(first, value(f0), value(f1))

    def spread(origin, p):
        tile = qbuf[origin, p]
        blank = jnp.zeros((rows, HEAD_DIM), jnp.bfloat16)
        return jnp.concatenate(
            [
                jnp.concatenate([tile[:rows], blank], axis=1),
                jnp.concatenate([blank, tile[rows:]], axis=1),
            ],
            axis=0,
        )

    def scores(origins, p):
        against = jnp.concatenate([spread(origin, p) for origin in origins], axis=0)
        keys = jnp.concatenate(
            [cbuf[f, :, 2 * j * HEAD_DIM : (2 * j + 1) * HEAD_DIM] for f, j in members(p)], axis=1
        )
        score = lax.dot_general(keys, against, NT, preferred_element_type=jnp.float32)
        score_new = lax.dot_general(kf[p], against, NT, preferred_element_type=jnp.float32)
        return score, score_new

    def weigh(origin, p, score, score_new):
        live = by_lane(p, lambda f: placed_ref[f] * blocks_ref[f])
        tiles = [score[a : a + BLOCK].reshape(-1, 8, lanes) for a in range(0, slots, BLOCK)]
        row = lax.broadcasted_iota(jnp.int32, (FRESH_ROWS, lanes), 0)
        counted = (row < tokens) & (me * tokens + row <= origin * tokens + lane_token)
        score_new = jnp.where(counted, score_new * factor, HIDDEN)
        top = jnp.max(score_new.reshape(-1, 8, lanes), axis=0)
        for b, tile in enumerate(tiles):
            top = jnp.maximum(top, jnp.where(b < live, jnp.max(tile, axis=0) * factor, HIDDEN))
        top = jnp.maximum(jnp.max(top, axis=0, keepdims=True), FLOOR)
        weight_new = jnp.exp2(score_new - top)
        total = jnp.sum(weight_new.reshape(-1, 8, lanes), axis=0)
        weights = []
        for b, tile in enumerate(tiles):
            shift = jnp.where(b < live, top, -HIDDEN)
            weight = jnp.exp2(tile * factor - shift[None])
            total = total + jnp.sum(weight, axis=0)
            weights.append(weight.reshape(BLOCK, lanes).astype(jnp.bfloat16))
        total = jnp.sum(total, axis=0, keepdims=True)
        return jnp.concatenate(weights, axis=0), weight_new.astype(jnp.bfloat16), top, total

    def partials(origins, p, score, score_new):
        parts = [
            weigh(
                origin, p, score[:, k * lanes : (k + 1) * lanes],
                score_new[:, k * lanes : (k + 1) * lanes],
            )
            for k, origin in enumerate(origins)
        ]
        weight = jnp.concatenate([part[0] for part in parts], axis=1)
        weight_new = jnp.concatenate([part[1] for part in parts], axis=1)
        both = jnp.dot(vt[p], weight, preferred_element_type=jnp.float32)
        both = both + lax.dot_general(vf[p], weight_new, TN, preferred_element_type=jnp.float32)
        return [
            (
                jnp.where(
                    first,
                    both[:HEAD_DIM, k * lanes : (k + 1) * lanes],
                    both[HEAD_DIM:, k * lanes : (k + 1) * lanes],
                ),
                part[2],
                part[3],
            )
            for k, part in enumerate(parts)
        ]

    def attend(origins, after=None):
        ahead = scores(origins, 0)
        for p in range(pairs):
            now = ahead
            if p + 1 < pairs:
                ahead = scores(origins, p + 1)
            for origin, part in zip(origins, partials(origins, p, *now)):
                pn[origin, p], ps[origin, p, 0:1], ps[origin, p, 1:2] = part
            if after is not None:
                after(p)

    def kept(d, p):
        return pn[d, p], ps[d, p, 0:1], ps[d, p, 1:2]

    def arrived(slot, p):
        numer = ci[slot, p].astype(jnp.int32).astype(jnp.float32) * cis[slot, p, 2:3]
        return numer, cis[slot, p, 0:1], cis[slot, p, 1:2]

    def merge(one, two):
        top = jnp.maximum(one[1], two[1])
        a = jnp.exp2(one[1] - top)
        b = jnp.exp2(two[1] - top)
        return a * one[0] + b * two[0], top, a * one[2] + b * two[2]

    def pack(d, p, part):
        numer, top, total = part
        reach = jnp.maximum(jnp.max(jnp.abs(numer), axis=0, keepdims=True), 1e-30)
        co[d, p] = jnp.round(numer * (STEPS / reach)).astype(jnp.int32).astype(jnp.int16)
        row = lax.broadcasted_iota(jnp.int32, (8, lanes), 0)
        cos[d, p] = jnp.where(row == 0, top, jnp.where(row == 1, total, reach * (1.0 / STEPS)))

    def chain_copies(d, c, side):
        target = me + 1 - 2 * side
        slot = jnp.where((d == target) & (side == 1), n, d)
        part = pl.ds(c * per, per)
        where = dict(device_id={"inst": target}, device_id_type=MESH)
        return (
            pltpu.make_async_remote_copy(
                src_ref=co.at[d, part], dst_ref=ci.at[slot, part],
                send_sem=c_send.at[d, c], recv_sem=c_recv.at[slot, c], **where
            ),
            pltpu.make_async_remote_copy(
                src_ref=cos.at[d, part], dst_ref=cis.at[slot, part],
                send_sem=s_send.at[d, c], recv_sem=s_recv.at[slot, c], **where
            ),
        )

    def chain_arrival(slot, c):
        part = pl.ds(c * per, per)
        pltpu.make_async_copy(ci.at[slot, part], ci.at[slot, part], c_recv.at[slot, c]).wait()
        pltpu.make_async_copy(cis.at[slot, part], cis.at[slot, part], s_recv.at[slot, c]).wait()

    at_end = (me == 0) | (me == n - 1)
    end_side = jnp.where(me == 0, 0, 1)

    def relay(t, chunks):
        for side in range(2):
            origin = me - t if side == 0 else me + t
            there = origin >= 0 if side == 0 else origin < n
            onward = me + 1 < n if side == 0 else me > 0

            @pl.when(there & onward)
            def _():
                for c in chunks:
                    q_copy(origin, c, side).wait_recv()
                    q_copy(origin, c, side).start()

    def relay_part(t, parts):
        size = -(-CHUNKS // parts)
        return lambda p: relay(t, range(min(p * size, CHUNKS), min((p + 1) * size, CHUNKS)))

    attend([me], relay_part(1, pairs))

    def advance(t, carry):
        @pl.when(t == n - 1)
        def _():
            for k in range(1, n):
                parcel(k).start()

        @pl.when(at_end & (t < n))
        def _():
            origin = me + t * (1 - 2 * end_side)
            for c in range(CHUNKS):
                q_copy(origin, c, 0).wait_recv()
                for p in range(c * per, (c + 1) * per):
                    pack(origin, p, partials([origin], p, *scores([origin], p))[0])
                for copy in chain_copies(origin, c, end_side):
                    copy.start()

        @pl.when(jnp.logical_not(at_end))
        def _():
            before, beyond = me - t >= 0, me + t < n

            @pl.when(before & beyond)
            def _():
                attend([me - t, me + t], relay_part(t + 1, pairs // 2))

            @pl.when(jnp.logical_not(before & beyond))
            def _():
                @pl.when(before | beyond)
                def _():
                    attend([jnp.where(before, me - t, me + t)])

                relay(t + 1, range(CHUNKS))

            for side in range(2):
                place = me if side == 0 else n - 1 - me
                far = t - place
                d = far if side == 0 else n - 1 - far

                @pl.when((far > place) & (far < n))
                def _():
                    for c in range(CHUNKS):
                        chain_arrival(d, c)
                        for p in range(c * per, (c + 1) * per):
                            pack(d, p, merge(kept(d, p), arrived(d, p)))
                        for copy in chain_copies(d, c, side):
                            copy.start()

        return carry

    lax.fori_loop(1, 2 * n - 1, advance, 0)

    for k in range(1, n):
        source = lax.rem(me + n - k, n)
        pltpu.make_async_copy(pi.at[source], pi.at[source], o_recv.at[source]).wait()
    gathered = [pi[i].astype(jnp.float32) for i in range(n)]
    for a in range(width_kv // HEAD_DIM):
        column = jnp.concatenate([x[a * tokens : (a + 1) * tokens] for x in gathered], axis=0)
        owned_ref[0, 0, :, a * HEAD_DIM : (a + 1) * HEAD_DIM] = column.astype(jnp.bfloat16)
    results = [pltpu.make_async_copy(owned_ref, owned_hbm, output_sem.at[2 * pairs])]
    results[0].start()

    for c in range(CHUNKS):
        for slot, there in ((me, me > 0), (n, me + 1 < n)):
            @pl.when(there)
            def _():
                chain_arrival(slot, c)
                for p in range(c * per, (c + 1) * per):
                    numer, top, total = merge(kept(me, p), arrived(slot, p))
                    pn[me, p] = numer
                    ps[me, p, 0:1] = top
                    ps[me, p, 1:2] = total

        for p in range(c * per, (c + 1) * per):
            numer, _, total = kept(me, p)
            span = by_lane(p, lambda f: span_ref[f])
            result = jnp.where(me * tokens + lane_token < span, numer / total, 0.0).T
            for h, (f, j) in enumerate(members(p)):
                for g in range(group):
                    at = (j * group + g) * HEAD_DIM
                    start = h * rows + g * tokens
                    att_ref[f, :, at : at + HEAD_DIM] = result[start : start + tokens].astype(
                        jnp.bfloat16
                    )
                span = pl.ds(j * group * HEAD_DIM, group * HEAD_DIM)
                result_copy = pltpu.make_async_copy(
                    att_ref.at[f, :, span], att_hbm.at[f, :, span], output_sem.at[2 * p + h]
                )
                result_copy.start()
                results.append(result_copy)

    for result_copy in results:
        result_copy.wait()
    for k in range(1, n):
        parcel(k).wait_send()
    for c in range(CHUNKS):
        for side in range(2):
            @pl.when(me + 1 < n if side == 0 else me > 0)
            def _():
                q_copy(me, c, side).wait_send()

    def drain(t, carry):
        for c in range(CHUNKS):
            for side in range(2):
                origin = me - t if side == 0 else me + t
                onward = me + 1 < n if side == 0 else me > 0

                @pl.when((origin >= 0 if side == 0 else origin < n) & onward)
                def _():
                    q_copy(origin, c, side).wait_send()

                d = me + t if side == 0 else me - t

                @pl.when(d < n if side == 0 else d >= 0)
                def _():
                    for copy in chain_copies(d, c, side):
                        copy.wait_send()
        return carry

    lax.fori_loop(1, n, drain, 0)


def hand_over(attended, owned, attended_out, owned_out, sem):
    copies = [
        pltpu.make_async_copy(attended, attended_out, sem.at[0]),
        pltpu.make_async_copy(owned, owned_out, sem.at[1]),
    ]
    for copy in copies:
        copy.start()
    for copy in copies:
        copy.wait()


def body(queries, tool_key_value, cache, placed, blocks, span_len, owner):
    n = lax.axis_size("inst")
    forks, tokens, width = queries.shape
    width_kv = tool_key_value.shape[2]
    slots = cache.shape[1]
    kv_heads = width_kv // (2 * HEAD_DIM)
    group = width // (kv_heads * HEAD_DIM)
    pairs = forks * kv_heads // 2
    lanes = 2 * group * tokens
    parcel = (n, tokens * width_kv // HEAD_DIM, HEAD_DIM)
    bf16, f32, i16 = jnp.bfloat16, jnp.float32, jnp.int16
    vmem, smem = pltpu.VMEM, pltpu.SMEM
    dma = pltpu.SemaphoreType.DMA
    work = n * pairs * slots * lanes
    attended, owned = pl.pallas_call(
        functools.partial(kernel, n),
        out_shape=(
            jax.ShapeDtypeStruct(queries.shape, bf16),
            jax.ShapeDtypeStruct((1, 1, n * tokens, width_kv), bf16),
        ),
        in_specs=[
            pl.BlockSpec(memory_space=pltpu.HBM)
        ]
        * 7,
        out_specs=(pl.BlockSpec(memory_space=pltpu.HBM),) * 2,
        scratch_shapes=[
            vmem(queries.shape, bf16),
            vmem((1, 1, n * tokens, width_kv), bf16),
            dma((2 * pairs + 1,)),
            vmem(queries.shape, bf16),
            vmem(tool_key_value.shape, bf16),
            smem((forks,), jnp.int32),
            smem((forks,), jnp.int32),
            smem((forks,), jnp.int32),
            smem((forks,), jnp.int32),
            dma((6,)),
            vmem(cache.shape, bf16),
            vmem((pairs, 2 * HEAD_DIM, slots), bf16),
            vmem((pairs, FRESH_ROWS, 2 * HEAD_DIM), bf16),
            vmem((pairs, FRESH_ROWS, 2 * HEAD_DIM), bf16),
            vmem((n, pairs, lanes, HEAD_DIM), bf16),
            vmem((n, pairs, HEAD_DIM, lanes), f32),
            vmem((n, pairs, 8, lanes), f32),
            vmem((n + 1, pairs, HEAD_DIM, lanes), i16),
            vmem((n + 1, pairs, 8, lanes), f32),
            vmem((n, pairs, HEAD_DIM, lanes), i16),
            vmem((n, pairs, 8, lanes), f32),
            vmem(parcel, bf16),
            vmem(parcel, bf16),
            dma((forks,)),
            dma((2, n, CHUNKS)),
            dma((n, CHUNKS)),
            dma((n, CHUNKS)),
            dma((n, CHUNKS)),
            dma((n + 1, CHUNKS)),
            dma((n + 1, CHUNKS)),
            dma((n,)),
            dma((n,)),
        ],
        compiler_params=pltpu.CompilerParams(
            collective_id=0, has_side_effects=True, vmem_limit_bytes=63 * 1024 * 1024
        ),
        cost_estimate=pl.CostEstimate(
            flops=work * 8 * HEAD_DIM, bytes_accessed=2 * cache.size, transcendentals=work
        ),
    )(queries, tool_key_value, cache, placed.reshape(-1), blocks.reshape(-1), span_len, owner)
    return pl.pallas_call(
        hand_over,
        out_shape=(
            jax.ShapeDtypeStruct(attended.shape, bf16),
            jax.ShapeDtypeStruct(owned.shape, bf16),
        ),
        in_specs=[pl.BlockSpec(memory_space=pltpu.HBM)] * 2,
        out_specs=(pl.BlockSpec(memory_space=pltpu.HBM),) * 2,
        scratch_shapes=[dma((2,))],
        compiler_params=pltpu.CompilerParams(vmem_limit_bytes=63 * 1024 * 1024),
    )(attended, owned)


def solution(mesh):
    return jax.shard_map(
        body,
        mesh=mesh,
        in_specs=(
            P(("groups", "rep"), "inst", "tp"),
            P(("groups", "rep"), "inst", "tp"),
            P(("groups", "rep"), "inst", "tp"),
            P(("groups", "rep"), "inst"),
            P(("groups", "rep"), "inst"),
            P(("groups", "rep")),
            P(("groups", "rep")),
        ),
        out_specs=(P(("groups", "rep"), "inst", "tp"), P(("groups", "inst"), "rep", None, "tp")),
        check_vma=False,
    )
```

```python
import functools
import math

import jax
import jax.numpy as jnp
from jax import lax
from jax.experimental import pallas as pl
from jax.experimental.pallas import tpu as pltpu
from jax.sharding import PartitionSpec as P

HEAD_DIM = 128
BLOCK = 128
FRESH_ROWS = 16
CHUNKS = 4
STEPS = 32000.0
LOG2E = 1.4426950408889634
HIDDEN = -1e30
FLOOR = -1e5
MESH = pl.DeviceIdType.MESH
NT = (((1,), (1,)), ((), ()))
TN = (((0,), (0,)), ((), ()))


def kernel(
    n, q_hbm, kv_hbm, cache_ref, placed_hbm, blocks_hbm, span_hbm, owner_hbm,
    att_ref, owned_ref,
    q_ref, kv_ref, placed_ref, blocks_ref, span_ref, owner_ref, input_sem,
    cbuf, vt, kf, vf, qbuf, pn, ps, ci, cis, co, cos, po, pi,
    cache_sem, q_send, q_recv, c_send, s_send, c_recv, s_recv, o_send, o_recv,
):
    forks, tokens, width = q_ref.shape
    width_kv = kv_ref.shape[2]
    kv_heads = width_kv // (2 * HEAD_DIM)
    group = width // (kv_heads * HEAD_DIM)
    rows = group * tokens
    lanes = 2 * rows
    pairs = forks * kv_heads // 2
    slots = cache_ref.shape[1]
    per = pairs // CHUNKS
    factor = LOG2E / math.sqrt(HEAD_DIM)
    me = lax.axis_index("inst")

    inputs = [
        pltpu.make_async_copy(source, target, input_sem.at[k])
        for k, (source, target) in enumerate(
            (
                (q_hbm, q_ref), (kv_hbm, kv_ref), (placed_hbm, placed_ref),
                (blocks_hbm, blocks_ref), (span_hbm, span_ref), (owner_hbm, owner_ref),
            )
        )
    ]
    for fetch in inputs:
        fetch.start()
    fetches = [
        pltpu.make_async_copy(cache_ref.at[f], cbuf.at[f], cache_sem.at[f])
        for f in range(forks)
    ]
    for fetch in fetches:
        fetch.start()

    barrier = pltpu.get_barrier_semaphore()
    for k in range(1, n):
        pl.semaphore_signal(
            barrier, inc=1, device_id={"inst": lax.rem(me + k, n)}, device_id_type=MESH
        )

    def members(p):
        return [(u // kv_heads, u % kv_heads) for u in (2 * p, 2 * p + 1)]

    inputs[0].wait()
    for p in range(pairs):
        parts = []
        for f, j in members(p):
            for g in range(group):
                at = (j * group + g) * HEAD_DIM
                parts.append(q_ref[f, :, at : at + HEAD_DIM].astype(jnp.float32))
        qbuf[me, p] = jnp.concatenate(parts, axis=0).astype(jnp.bfloat16)

    pl.semaphore_wait(barrier, n - 1)

    def q_copy(origin, c, side):
        part = qbuf.at[origin, pl.ds(c * per, per)]
        return pltpu.make_async_remote_copy(
            src_ref=part, dst_ref=part,
            send_sem=q_send.at[side, origin, c], recv_sem=q_recv.at[origin, c],
            device_id={"inst": me + 1 if side == 0 else me - 1}, device_id_type=MESH,
        )

    for c in range(CHUNKS):
        for side in range(2):
            @pl.when(me + 1 < n if side == 0 else me > 0)
            def _():
                q_copy(me, c, side).start()

    for fetch in inputs[1:]:
        fetch.wait()
    for i in range(n):
        chosen = None
        for f in range(forks):
            tile = kv_ref[f].astype(jnp.float32)
            token = me * tokens + lax.broadcasted_iota(jnp.int32, tile.shape, 0)
            keep = (token < span_ref[f]) & (jnp.broadcast_to(owner_ref[f], tile.shape) == i)
            tile = jnp.where(keep, tile, 0.0)
            chosen = tile if chosen is None else chosen + tile
        po[i] = jnp.concatenate(
            [chosen[:, a : a + HEAD_DIM] for a in range(0, width_kv, HEAD_DIM)], axis=0
        ).astype(jnp.bfloat16)
    pi[me] = po[me]

    def parcel(k):
        target = lax.rem(me + k, n)
        return pltpu.make_async_remote_copy(
            src_ref=po.at[target], dst_ref=pi.at[me],
            send_sem=o_send.at[target], recv_sem=o_recv.at[me],
            device_id={"inst": target}, device_id_type=MESH,
        )

    for p in range(pairs):
        for ref, shift in ((kf, 0), (vf, HEAD_DIM)):
            both = [
                kv_ref[f, :, 2 * j * HEAD_DIM + shift : 2 * j * HEAD_DIM + shift + HEAD_DIM]
                for f, j in members(p)
            ]
            tile = jnp.concatenate(both, axis=1).astype(jnp.float32)
            pad = jnp.zeros((FRESH_ROWS - tokens, 2 * HEAD_DIM), jnp.float32)
            ref[p] = jnp.concatenate([tile, pad], axis=0).astype(jnp.bfloat16)

    for fetch in fetches:
        fetch.wait()
    for p in range(pairs):
        for h, (f, j) in enumerate(members(p)):
            at = (2 * j + 1) * HEAD_DIM
            vt[p, h * HEAD_DIM : (h + 1) * HEAD_DIM, :] = cbuf[f, :, at : at + HEAD_DIM].T

    lane = lax.broadcasted_iota(jnp.int32, (1, lanes), 1)
    lane_token = lax.rem(lane, tokens)
    first = lane < rows

    def by_lane(p, value):
        (f0, _), (f1, _) = members(p)
        return jnp.where(first, value(f0), value(f1))

    def spread(origin, p):
        tile = qbuf[origin, p]
        blank = jnp.zeros((rows, HEAD_DIM), jnp.bfloat16)
        return jnp.concatenate(
            [
                jnp.concatenate([tile[:rows], blank], axis=1),
                jnp.concatenate([blank, tile[rows:]], axis=1),
            ],
            axis=0,
        )

    def scores(origins, p):
        against = jnp.concatenate([spread(origin, p) for origin in origins], axis=0)
        keys = jnp.concatenate(
            [cbuf[f, :, 2 * j * HEAD_DIM : (2 * j + 1) * HEAD_DIM] for f, j in members(p)], axis=1
        )
        score = lax.dot_general(keys, against, NT, preferred_element_type=jnp.float32)
        score_new = lax.dot_general(kf[p], against, NT, preferred_element_type=jnp.float32)
        return score, score_new

    def weigh(origin, p, score, score_new):
        live = by_lane(p, lambda f: placed_ref[f] * blocks_ref[f])
        tiles = [score[a : a + BLOCK].reshape(-1, 8, lanes) for a in range(0, slots, BLOCK)]
        row = lax.broadcasted_iota(jnp.int32, (FRESH_ROWS, lanes), 0)
        counted = (row < tokens) & (me * tokens + row <= origin * tokens + lane_token)
        score_new = jnp.where(counted, score_new * factor, HIDDEN)
        top = jnp.max(score_new.reshape(-1, 8, lanes), axis=0)
        for b, tile in enumerate(tiles):
            top = jnp.maximum(top, jnp.where(b < live, jnp.max(tile, axis=0) * factor, HIDDEN))
        top = jnp.maximum(jnp.max(top, axis=0, keepdims=True), FLOOR)
        weight_new = jnp.exp2(score_new - top)
        total = jnp.sum(weight_new.reshape(-1, 8, lanes), axis=0)
        weights = []
        for b, tile in enumerate(tiles):
            shift = jnp.where(b < live, top, -HIDDEN)
            weight = jnp.exp2(tile * factor - shift[None])
            total = total + jnp.sum(weight, axis=0)
            weights.append(weight.reshape(BLOCK, lanes).astype(jnp.bfloat16))
        total = jnp.sum(total, axis=0, keepdims=True)
        return jnp.concatenate(weights, axis=0), weight_new.astype(jnp.bfloat16), top, total

    def partials(origins, p, score, score_new):
        parts = [
            weigh(
                origin, p, score[:, k * lanes : (k + 1) * lanes],
                score_new[:, k * lanes : (k + 1) * lanes],
            )
            for k, origin in enumerate(origins)
        ]
        weight = jnp.concatenate([part[0] for part in parts], axis=1)
        weight_new = jnp.concatenate([part[1] for part in parts], axis=1)
        both = jnp.dot(vt[p], weight, preferred_element_type=jnp.float32)
        both = both + lax.dot_general(vf[p], weight_new, TN, preferred_element_type=jnp.float32)
        return [
            (
                jnp.where(
                    first,
                    both[:HEAD_DIM, k * lanes : (k + 1) * lanes],
                    both[HEAD_DIM:, k * lanes : (k + 1) * lanes],
                ),
                part[2],
                part[3],
            )
            for k, part in enumerate(parts)
        ]

    def attend(origins, after=None):
        ahead = scores(origins, 0)
        for p in range(pairs):
            now = ahead
            if p + 1 < pairs:
                ahead = scores(origins, p + 1)
            for origin, part in zip(origins, partials(origins, p, *now)):
                pn[origin, p], ps[origin, p, 0:1], ps[origin, p, 1:2] = part
            if after is not None:
                after(p)

    def kept(d, p):
        return pn[d, p], ps[d, p, 0:1], ps[d, p, 1:2]

    def arrived(slot, p):
        numer = ci[slot, p].astype(jnp.int32).astype(jnp.float32) * cis[slot, p, 2:3]
        return numer, cis[slot, p, 0:1], cis[slot, p, 1:2]

    def merge(one, two):
        top = jnp.maximum(one[1], two[1])
        a = jnp.exp2(one[1] - top)
        b = jnp.exp2(two[1] - top)
        return a * one[0] + b * two[0], top, a * one[2] + b * two[2]

    def pack(d, p, part):
        numer, top, total = part
        reach = jnp.maximum(jnp.max(jnp.abs(numer), axis=0, keepdims=True), 1e-30)
        co[d, p] = jnp.round(numer * (STEPS / reach)).astype(jnp.int32).astype(jnp.int16)
        row = lax.broadcasted_iota(jnp.int32, (8, lanes), 0)
        cos[d, p] = jnp.where(row == 0, top, jnp.where(row == 1, total, reach * (1.0 / STEPS)))

    def chain_copies(d, c, side):
        target = me + 1 - 2 * side
        slot = jnp.where((d == target) & (side == 1), n, d)
        part = pl.ds(c * per, per)
        where = dict(device_id={"inst": target}, device_id_type=MESH)
        return (
            pltpu.make_async_remote_copy(
                src_ref=co.at[d, part], dst_ref=ci.at[slot, part],
                send_sem=c_send.at[d, c], recv_sem=c_recv.at[slot, c], **where
            ),
            pltpu.make_async_remote_copy(
                src_ref=cos.at[d, part], dst_ref=cis.at[slot, part],
                send_sem=s_send.at[d, c], recv_sem=s_recv.at[slot, c], **where
            ),
        )

    def chain_arrival(slot, c):
        part = pl.ds(c * per, per)
        pltpu.make_async_copy(ci.at[slot, part], ci.at[slot, part], c_recv.at[slot, c]).wait()
        pltpu.make_async_copy(cis.at[slot, part], cis.at[slot, part], s_recv.at[slot, c]).wait()

    at_end = (me == 0) | (me == n - 1)
    end_side = jnp.where(me == 0, 0, 1)

    def relay(t, chunks):
        for side in range(2):
            origin = me - t if side == 0 else me + t
            there = origin >= 0 if side == 0 else origin < n
            onward = me + 1 < n if side == 0 else me > 0

            @pl.when(there & onward)
            def _():
                for c in chunks:
                    q_copy(origin, c, side).wait_recv()
                    q_copy(origin, c, side).start()

    def relay_part(t, parts):
        size = -(-CHUNKS // parts)
        return lambda p: relay(t, range(min(p * size, CHUNKS), min((p + 1) * size, CHUNKS)))

    attend([me], relay_part(1, pairs))

    def advance(t, carry):
        @pl.when(t == n - 1)
        def _():
            for k in range(1, n):
                parcel(k).start()

        @pl.when(at_end & (t < n))
        def _():
            origin = me + t * (1 - 2 * end_side)

            def arrive(c):
                q_copy(origin, c, 0).wait_recv()
                return [(p, scores([origin], p)) for p in range(c * per, (c + 1) * per)]

            ahead = arrive(0)
            for c in range(CHUNKS):
                now = ahead
                if c + 1 < CHUNKS:
                    ahead = arrive(c + 1)
                for p, score in now:
                    pack(origin, p, partials([origin], p, *score)[0])
                for copy in chain_copies(origin, c, end_side):
                    copy.start()

        @pl.when(jnp.logical_not(at_end))
        def _():
            before, beyond = me - t >= 0, me + t < n

            @pl.when(before & beyond)
            def _():
                attend([me - t, me + t], relay_part(t + 1, pairs // 2))

            @pl.when(jnp.logical_not(before & beyond))
            def _():
                @pl.when(before | beyond)
                def _():
                    attend([jnp.where(before, me - t, me + t)])

                relay(t + 1, range(CHUNKS))

            for side in range(2):
                place = me if side == 0 else n - 1 - me
                far = t - place
                d = far if side == 0 else n - 1 - far

                @pl.when((far > place) & (far < n))
                def _():
                    for c in range(CHUNKS):
                        chain_arrival(d, c)
                        for p in range(c * per, (c + 1) * per):
                            pack(d, p, merge(kept(d, p), arrived(d, p)))
                        for copy in chain_copies(d, c, side):
                            copy.start()

        return carry

    lax.fori_loop(1, 2 * n - 1, advance, 0)

    for k in range(1, n):
        source = lax.rem(me + n - k, n)
        pltpu.make_async_copy(pi.at[source], pi.at[source], o_recv.at[source]).wait()
    gathered = [pi[i].astype(jnp.float32) for i in range(n)]
    for a in range(width_kv // HEAD_DIM):
        column = jnp.concatenate([x[a * tokens : (a + 1) * tokens] for x in gathered], axis=0)
        owned_ref[0, 0, :, a * HEAD_DIM : (a + 1) * HEAD_DIM] = column.astype(jnp.bfloat16)

    for c in range(CHUNKS):
        for slot, there in ((me, me > 0), (n, me + 1 < n)):
            @pl.when(there)
            def _():
                chain_arrival(slot, c)
                for p in range(c * per, (c + 1) * per):
                    numer, top, total = merge(kept(me, p), arrived(slot, p))
                    pn[me, p] = numer
                    ps[me, p, 0:1] = top
                    ps[me, p, 1:2] = total

        for p in range(c * per, (c + 1) * per):
            numer, _, total = kept(me, p)
            span = by_lane(p, lambda f: span_ref[f])
            result = jnp.where(me * tokens + lane_token < span, numer / total, 0.0).T
            for h, (f, j) in enumerate(members(p)):
                for g in range(group):
                    at = (j * group + g) * HEAD_DIM
                    start = h * rows + g * tokens
                    att_ref[f, :, at : at + HEAD_DIM] = result[start : start + tokens].astype(
                        jnp.bfloat16
                    )

    for k in range(1, n):
        parcel(k).wait_send()
    for c in range(CHUNKS):
        for side in range(2):
            @pl.when(me + 1 < n if side == 0 else me > 0)
            def _():
                q_copy(me, c, side).wait_send()

    def drain(t, carry):
        for c in range(CHUNKS):
            for side in range(2):
                origin = me - t if side == 0 else me + t
                onward = me + 1 < n if side == 0 else me > 0

                @pl.when((origin >= 0 if side == 0 else origin < n) & onward)
                def _():
                    q_copy(origin, c, side).wait_send()

                d = me + t if side == 0 else me - t

                @pl.when(d < n if side == 0 else d >= 0)
                def _():
                    for copy in chain_copies(d, c, side):
                        copy.wait_send()
        return carry

    lax.fori_loop(1, n, drain, 0)


def hand_over(attended, owned, attended_out, owned_out):
    attended_out[...] = attended[...]
    owned_out[...] = owned[...]


def body(queries, tool_key_value, cache, placed, blocks, span_len, owner):
    n = lax.axis_size("inst")
    forks, tokens, width = queries.shape
    width_kv = tool_key_value.shape[2]
    slots = cache.shape[1]
    kv_heads = width_kv // (2 * HEAD_DIM)
    group = width // (kv_heads * HEAD_DIM)
    pairs = forks * kv_heads // 2
    lanes = 2 * group * tokens
    parcel = (n, tokens * width_kv // HEAD_DIM, HEAD_DIM)
    bf16, f32, i16 = jnp.bfloat16, jnp.float32, jnp.int16
    vmem, smem = pltpu.VMEM, pltpu.SMEM
    dma = pltpu.SemaphoreType.DMA
    work = n * pairs * slots * lanes
    attended, owned = pl.pallas_call(
        functools.partial(kernel, n),
        out_shape=(
            jax.ShapeDtypeStruct(queries.shape, bf16),
            jax.ShapeDtypeStruct((1, 1, n * tokens, width_kv), bf16),
        ),
        in_specs=[
            pl.BlockSpec(memory_space=pltpu.HBM)
        ]
        * 7,
        out_specs=(pl.BlockSpec(memory_space=vmem), pl.BlockSpec(memory_space=vmem)),
        scratch_shapes=[
            vmem(queries.shape, bf16),
            vmem(tool_key_value.shape, bf16),
            smem((forks,), jnp.int32),
            smem((forks,), jnp.int32),
            smem((forks,), jnp.int32),
            smem((forks,), jnp.int32),
            dma((6,)),
            vmem(cache.shape, bf16),
            vmem((pairs, 2 * HEAD_DIM, slots), bf16),
            vmem((pairs, FRESH_ROWS, 2 * HEAD_DIM), bf16),
            vmem((pairs, FRESH_ROWS, 2 * HEAD_DIM), bf16),
            vmem((n, pairs, lanes, HEAD_DIM), bf16),
            vmem((n, pairs, HEAD_DIM, lanes), f32),
            vmem((n, pairs, 8, lanes), f32),
            vmem((n + 1, pairs, HEAD_DIM, lanes), i16),
            vmem((n + 1, pairs, 8, lanes), f32),
            vmem((n, pairs, HEAD_DIM, lanes), i16),
            vmem((n, pairs, 8, lanes), f32),
            vmem(parcel, bf16),
            vmem(parcel, bf16),
            dma((forks,)),
            dma((2, n, CHUNKS)),
            dma((n, CHUNKS)),
            dma((n, CHUNKS)),
            dma((n, CHUNKS)),
            dma((n + 1, CHUNKS)),
            dma((n + 1, CHUNKS)),
            dma((n,)),
            dma((n,)),
        ],
        compiler_params=pltpu.CompilerParams(
            collective_id=0, has_side_effects=True, vmem_limit_bytes=63 * 1024 * 1024
        ),
        cost_estimate=pl.CostEstimate(
            flops=work * 8 * HEAD_DIM, bytes_accessed=2 * cache.size, transcendentals=work
        ),
    )(queries, tool_key_value, cache, placed.reshape(-1), blocks.reshape(-1), span_len, owner)
    return pl.pallas_call(
        hand_over,
        out_shape=(
            jax.ShapeDtypeStruct(attended.shape, bf16),
            jax.ShapeDtypeStruct(owned.shape, bf16),
        ),
        in_specs=[pl.BlockSpec(memory_space=vmem)] * 2,
        out_specs=(pl.BlockSpec(memory_space=vmem),) * 2,
        compiler_params=pltpu.CompilerParams(vmem_limit_bytes=63 * 1024 * 1024),
    )(attended, owned)


def solution(mesh):
    return jax.shard_map(
        body,
        mesh=mesh,
        in_specs=(
            P(("groups", "rep"), "inst", "tp"),
            P(("groups", "rep"), "inst", "tp"),
            P(("groups", "rep"), "inst", "tp"),
            P(("groups", "rep"), "inst"),
            P(("groups", "rep"), "inst"),
            P(("groups", "rep")),
            P(("groups", "rep")),
        ),
        out_specs=(P(("groups", "rep"), "inst", "tp"), P(("groups", "inst"), "rep", None, "tp")),
        check_vma=False,
    )
```

```python
import functools
import math

import jax
import jax.numpy as jnp
from jax import lax
from jax.experimental import pallas as pl
from jax.experimental.pallas import tpu as pltpu
from jax.sharding import PartitionSpec as P

HEAD_DIM = 128
BLOCK = 128
FRESH_ROWS = 16
CHUNKS = 4
STEPS = 32000.0
LOG2E = 1.4426950408889634
HIDDEN = -1e30
FLOOR = -1e5
MESH = pl.DeviceIdType.MESH
NT = (((1,), (1,)), ((), ()))
TN = (((0,), (0,)), ((), ()))


def kernel(
    n, q_hbm, kv_hbm, cache_ref, placed_hbm, blocks_hbm, span_hbm, owner_hbm,
    att_ref, owned_ref,
    q_ref, kv_ref, placed_ref, blocks_ref, span_ref, owner_ref, input_sem,
    cbuf, vt, kf, vf, qbuf, pn, ps, ci, cis, co, cos, po, pi,
    cache_sem, q_send, q_recv, c_send, s_send, c_recv, s_recv, o_send, o_recv,
):
    forks, tokens, width = q_ref.shape
    width_kv = kv_ref.shape[2]
    kv_heads = width_kv // (2 * HEAD_DIM)
    group = width // (kv_heads * HEAD_DIM)
    rows = group * tokens
    lanes = 2 * rows
    pairs = forks * kv_heads // 2
    slots = cache_ref.shape[1]
    per = pairs // CHUNKS
    factor = LOG2E / math.sqrt(HEAD_DIM)
    me = lax.axis_index("inst")

    inputs = [
        pltpu.make_async_copy(source, target, input_sem.at[k])
        for k, (source, target) in enumerate(
            (
                (q_hbm, q_ref), (kv_hbm, kv_ref), (placed_hbm, placed_ref),
                (blocks_hbm, blocks_ref), (span_hbm, span_ref), (owner_hbm, owner_ref),
            )
        )
    ]
    for fetch in inputs:
        fetch.start()
    fetches = [
        pltpu.make_async_copy(cache_ref.at[f], cbuf.at[f], cache_sem.at[f])
        for f in range(forks)
    ]
    for fetch in fetches:
        fetch.start()

    barrier = pltpu.get_barrier_semaphore()
    for k in range(1, n):
        pl.semaphore_signal(
            barrier, inc=1, device_id={"inst": lax.rem(me + k, n)}, device_id_type=MESH
        )

    def members(p):
        return [(u // kv_heads, u % kv_heads) for u in (2 * p, 2 * p + 1)]

    inputs[0].wait()
    for p in range(pairs):
        parts = []
        for f, j in members(p):
            for g in range(group):
                at = (j * group + g) * HEAD_DIM
                parts.append(q_ref[f, :, at : at + HEAD_DIM].astype(jnp.float32))
        qbuf[me, p] = jnp.concatenate(parts, axis=0).astype(jnp.bfloat16)

    pl.semaphore_wait(barrier, n - 1)

    def q_copy(origin, c, side):
        part = qbuf.at[origin, pl.ds(c * per, per)]
        return pltpu.make_async_remote_copy(
            src_ref=part, dst_ref=part,
            send_sem=q_send.at[side, origin, c], recv_sem=q_recv.at[origin, c],
            device_id={"inst": me + 1 if side == 0 else me - 1}, device_id_type=MESH,
        )

    for c in range(CHUNKS):
        for side in range(2):
            @pl.when(me + 1 < n if side == 0 else me > 0)
            def _():
                q_copy(me, c, side).start()

    for fetch in inputs[1:]:
        fetch.wait()
    for i in range(n):
        chosen = None
        for f in range(forks):
            tile = kv_ref[f].astype(jnp.float32)
            token = me * tokens + lax.broadcasted_iota(jnp.int32, tile.shape, 0)
            keep = (token < span_ref[f]) & (jnp.broadcast_to(owner_ref[f], tile.shape) == i)
            tile = jnp.where(keep, tile, 0.0)
            chosen = tile if chosen is None else chosen + tile
        po[i] = jnp.concatenate(
            [chosen[:, a : a + HEAD_DIM] for a in range(0, width_kv, HEAD_DIM)], axis=0
        ).astype(jnp.bfloat16)
    pi[me] = po[me]

    def parcel(k):
        target = lax.rem(me + k, n)
        return pltpu.make_async_remote_copy(
            src_ref=po.at[target], dst_ref=pi.at[me],
            send_sem=o_send.at[target], recv_sem=o_recv.at[me],
            device_id={"inst": target}, device_id_type=MESH,
        )

    for p in range(pairs):
        for ref, shift in ((kf, 0), (vf, HEAD_DIM)):
            both = [
                kv_ref[f, :, 2 * j * HEAD_DIM + shift : 2 * j * HEAD_DIM + shift + HEAD_DIM]
                for f, j in members(p)
            ]
            tile = jnp.concatenate(both, axis=1).astype(jnp.float32)
            pad = jnp.zeros((FRESH_ROWS - tokens, 2 * HEAD_DIM), jnp.float32)
            ref[p] = jnp.concatenate([tile, pad], axis=0).astype(jnp.bfloat16)

    for fetch in fetches:
        fetch.wait()
    for p in range(pairs):
        for h, (f, j) in enumerate(members(p)):
            at = (2 * j + 1) * HEAD_DIM
            vt[p, h * HEAD_DIM : (h + 1) * HEAD_DIM, :] = cbuf[f, :, at : at + HEAD_DIM].T

    lane = lax.broadcasted_iota(jnp.int32, (1, lanes), 1)
    lane_token = lax.rem(lane, tokens)
    first = lane < rows

    def by_lane(p, value):
        (f0, _), (f1, _) = members(p)
        return jnp.where(first, value(f0), value(f1))

    def spread(origin, p):
        tile = qbuf[origin, p]
        blank = jnp.zeros((rows, HEAD_DIM), jnp.bfloat16)
        return jnp.concatenate(
            [
                jnp.concatenate([tile[:rows], blank], axis=1),
                jnp.concatenate([blank, tile[rows:]], axis=1),
            ],
            axis=0,
        )

    def scores(origins, p):
        against = jnp.concatenate([spread(origin, p) for origin in origins], axis=0)
        keys = jnp.concatenate(
            [cbuf[f, :, 2 * j * HEAD_DIM : (2 * j + 1) * HEAD_DIM] for f, j in members(p)], axis=1
        )
        score = lax.dot_general(keys, against, NT, preferred_element_type=jnp.float32)
        score_new = lax.dot_general(kf[p], against, NT, preferred_element_type=jnp.float32)
        return score, score_new

    def weigh(origin, p, score, score_new):
        live = by_lane(p, lambda f: placed_ref[f] * blocks_ref[f])
        tiles = [score[a : a + BLOCK].reshape(-1, 8, lanes) for a in range(0, slots, BLOCK)]
        row = lax.broadcasted_iota(jnp.int32, (FRESH_ROWS, lanes), 0)
        counted = (row < tokens) & (me * tokens + row <= origin * tokens + lane_token)
        score_new = jnp.where(counted, score_new * factor, HIDDEN)
        top = jnp.max(score_new.reshape(-1, 8, lanes), axis=0)
        for b, tile in enumerate(tiles):
            top = jnp.maximum(top, jnp.where(b < live, jnp.max(tile, axis=0) * factor, HIDDEN))
        top = jnp.maximum(jnp.max(top, axis=0, keepdims=True), FLOOR)
        weight_new = jnp.exp2(score_new - top)
        total = jnp.sum(weight_new.reshape(-1, 8, lanes), axis=0)
        weights = []
        for b, tile in enumerate(tiles):
            shift = jnp.where(b < live, top, -HIDDEN)
            weight = jnp.exp2(tile * factor - shift[None])
            total = total + jnp.sum(weight, axis=0)
            weights.append(weight.reshape(BLOCK, lanes).astype(jnp.bfloat16))
        total = jnp.sum(total, axis=0, keepdims=True)
        return jnp.concatenate(weights, axis=0), weight_new.astype(jnp.bfloat16), top, total

    def partials(origins, p, score, score_new):
        parts = [
            weigh(
                origin, p, score[:, k * lanes : (k + 1) * lanes],
                score_new[:, k * lanes : (k + 1) * lanes],
            )
            for k, origin in enumerate(origins)
        ]
        weight = jnp.concatenate([part[0] for part in parts], axis=1)
        weight_new = jnp.concatenate([part[1] for part in parts], axis=1)
        both = jnp.dot(vt[p], weight, preferred_element_type=jnp.float32)
        both = both + lax.dot_general(vf[p], weight_new, TN, preferred_element_type=jnp.float32)
        return [
            (
                jnp.where(
                    first,
                    both[:HEAD_DIM, k * lanes : (k + 1) * lanes],
                    both[HEAD_DIM:, k * lanes : (k + 1) * lanes],
                ),
                part[2],
                part[3],
            )
            for k, part in enumerate(parts)
        ]

    def attend(origins, after=None):
        ahead = scores(origins, 0)
        for p in range(pairs):
            now = ahead
            if p + 1 < pairs:
                ahead = scores(origins, p + 1)
            for origin, part in zip(origins, partials(origins, p, *now)):
                pn[origin, p], ps[origin, p, 0:1], ps[origin, p, 1:2] = part
            if after is not None:
                after(p)

    def kept(d, p):
        return pn[d, p], ps[d, p, 0:1], ps[d, p, 1:2]

    def arrived(slot, p):
        numer = ci[slot, p].astype(jnp.int32).astype(jnp.float32) * cis[slot, p, 2:3]
        return numer, cis[slot, p, 0:1], cis[slot, p, 1:2]

    def merge(one, two):
        top = jnp.maximum(one[1], two[1])
        a = jnp.exp2(one[1] - top)
        b = jnp.exp2(two[1] - top)
        return a * one[0] + b * two[0], top, a * one[2] + b * two[2]

    def pack(d, p, part):
        numer, top, total = part
        reach = jnp.maximum(jnp.max(jnp.abs(numer), axis=0, keepdims=True), 1e-30)
        co[d, p] = jnp.round(numer * (STEPS / reach)).astype(jnp.int32).astype(jnp.int16)
        row = lax.broadcasted_iota(jnp.int32, (8, lanes), 0)
        cos[d, p] = jnp.where(row == 0, top, jnp.where(row == 1, total, reach * (1.0 / STEPS)))

    def chain_copies(d, c, side):
        target = me + 1 - 2 * side
        slot = jnp.where((d == target) & (side == 1), n, d)
        part = pl.ds(c * per, per)
        where = dict(device_id={"inst": target}, device_id_type=MESH)
        return (
            pltpu.make_async_remote_copy(
                src_ref=co.at[d, part], dst_ref=ci.at[slot, part],
                send_sem=c_send.at[d, c], recv_sem=c_recv.at[slot, c], **where
            ),
            pltpu.make_async_remote_copy(
                src_ref=cos.at[d, part], dst_ref=cis.at[slot, part],
                send_sem=s_send.at[d, c], recv_sem=s_recv.at[slot, c], **where
            ),
        )

    def chain_arrival(slot, c):
        part = pl.ds(c * per, per)
        pltpu.make_async_copy(ci.at[slot, part], ci.at[slot, part], c_recv.at[slot, c]).wait()
        pltpu.make_async_copy(cis.at[slot, part], cis.at[slot, part], s_recv.at[slot, c]).wait()

    at_end = (me == 0) | (me == n - 1)
    end_side = jnp.where(me == 0, 0, 1)

    def relay(t, chunks):
        for side in range(2):
            origin = me - t if side == 0 else me + t
            there = origin >= 0 if side == 0 else origin < n
            onward = me + 1 < n if side == 0 else me > 0

            @pl.when(there & onward)
            def _():
                for c in chunks:
                    q_copy(origin, c, side).wait_recv()
                    q_copy(origin, c, side).start()

    def relay_part(t, parts):
        size = -(-CHUNKS // parts)
        return lambda p: relay(
            t, range(min(1 + p * size, CHUNKS), min(1 + (p + 1) * size, CHUNKS))
        )

    def chain_step(d, c, side):
        chain_arrival(d, c)
        for p in range(c * per, (c + 1) * per):
            pack(d, p, merge(kept(d, p), arrived(d, p)))
        for copy in chain_copies(d, c, side):
            copy.start()

    relay(1, range(1))
    attend([me], relay_part(1, pairs))

    def advance(t, carry):
        @pl.when(t == n - 1)
        def _():
            for k in range(1, n):
                parcel(k).start()

        @pl.when(at_end & (t < n))
        def _():
            origin = me + t * (1 - 2 * end_side)

            def arrive(c):
                q_copy(origin, c, 0).wait_recv()
                return [(p, scores([origin], p)) for p in range(c * per, (c + 1) * per)]

            ahead = arrive(0)
            for c in range(CHUNKS):
                now = ahead
                if c + 1 < CHUNKS:
                    ahead = arrive(c + 1)
                for p, score in now:
                    pack(origin, p, partials([origin], p, *score)[0])
                for copy in chain_copies(origin, c, end_side):
                    copy.start()

        @pl.when(jnp.logical_not(at_end))
        def _():
            before, beyond = me - t >= 0, me + t < n

            @pl.when(before & beyond)
            def _():
                relay(t + 1, range(1))
                attend([me - t, me + t], relay_part(t + 1, pairs // 2))

            @pl.when(jnp.logical_not(before & beyond))
            def _():
                @pl.when(before | beyond)
                def _():
                    origin = jnp.where(before, me - t, me + t)
                    side = jnp.where(before, 1, 0)
                    prompt = jnp.where(before, me == n - 2, me == 1)

                    def after(p):
                        if (p + 1) % per == 0:
                            @pl.when(prompt)
                            def _():
                                chain_step(origin, p // per, side)

                    attend([origin], after)

                relay(t + 1, range(CHUNKS))

            for side in range(2):
                place = me if side == 0 else n - 1 - me
                far = t - place
                d = far if side == 0 else n - 1 - far

                done = (place == 1) & (far > place + 1)

                @pl.when((far > place) & (far < n) & jnp.logical_not(done))
                def _():
                    for c in range(CHUNKS):
                        chain_step(d, c, side)

        return carry

    lax.fori_loop(1, 2 * n - 1, advance, 0)

    for k in range(1, n):
        source = lax.rem(me + n - k, n)
        pltpu.make_async_copy(pi.at[source], pi.at[source], o_recv.at[source]).wait()
    gathered = [pi[i].astype(jnp.float32) for i in range(n)]
    for a in range(width_kv // HEAD_DIM):
        column = jnp.concatenate([x[a * tokens : (a + 1) * tokens] for x in gathered], axis=0)
        owned_ref[0, 0, :, a * HEAD_DIM : (a + 1) * HEAD_DIM] = column.astype(jnp.bfloat16)

    for c in range(CHUNKS):
        for slot, there in ((me, me > 0), (n, me + 1 < n)):
            @pl.when(there)
            def _():
                chain_arrival(slot, c)
                for p in range(c * per, (c + 1) * per):
                    numer, top, total = merge(kept(me, p), arrived(slot, p))
                    pn[me, p] = numer
                    ps[me, p, 0:1] = top
                    ps[me, p, 1:2] = total

        for p in range(c * per, (c + 1) * per):
            numer, _, total = kept(me, p)
            span = by_lane(p, lambda f: span_ref[f])
            result = jnp.where(me * tokens + lane_token < span, numer / total, 0.0).T
            for h, (f, j) in enumerate(members(p)):
                for g in range(group):
                    at = (j * group + g) * HEAD_DIM
                    start = h * rows + g * tokens
                    att_ref[f, :, at : at + HEAD_DIM] = result[start : start + tokens].astype(
                        jnp.bfloat16
                    )

    for k in range(1, n):
        parcel(k).wait_send()
    for c in range(CHUNKS):
        for side in range(2):
            @pl.when(me + 1 < n if side == 0 else me > 0)
            def _():
                q_copy(me, c, side).wait_send()

    def drain(t, carry):
        for c in range(CHUNKS):
            for side in range(2):
                origin = me - t if side == 0 else me + t
                onward = me + 1 < n if side == 0 else me > 0

                @pl.when((origin >= 0 if side == 0 else origin < n) & onward)
                def _():
                    q_copy(origin, c, side).wait_send()

                d = me + t if side == 0 else me - t

                @pl.when(d < n if side == 0 else d >= 0)
                def _():
                    for copy in chain_copies(d, c, side):
                        copy.wait_send()
        return carry

    lax.fori_loop(1, n, drain, 0)


def hand_over(attended, owned, attended_out, owned_out):
    attended_out[...] = attended[...]
    owned_out[...] = owned[...]


def body(queries, tool_key_value, cache, placed, blocks, span_len, owner):
    n = lax.axis_size("inst")
    forks, tokens, width = queries.shape
    width_kv = tool_key_value.shape[2]
    slots = cache.shape[1]
    kv_heads = width_kv // (2 * HEAD_DIM)
    group = width // (kv_heads * HEAD_DIM)
    pairs = forks * kv_heads // 2
    lanes = 2 * group * tokens
    parcel = (n, tokens * width_kv // HEAD_DIM, HEAD_DIM)
    bf16, f32, i16 = jnp.bfloat16, jnp.float32, jnp.int16
    vmem, smem = pltpu.VMEM, pltpu.SMEM
    dma = pltpu.SemaphoreType.DMA
    work = n * pairs * slots * lanes
    attended, owned = pl.pallas_call(
        functools.partial(kernel, n),
        out_shape=(
            jax.ShapeDtypeStruct(queries.shape, bf16),
            jax.ShapeDtypeStruct((1, 1, n * tokens, width_kv), bf16),
        ),
        in_specs=[
            pl.BlockSpec(memory_space=pltpu.HBM)
        ]
        * 7,
        out_specs=(pl.BlockSpec(memory_space=vmem), pl.BlockSpec(memory_space=vmem)),
        scratch_shapes=[
            vmem(queries.shape, bf16),
            vmem(tool_key_value.shape, bf16),
            smem((forks,), jnp.int32),
            smem((forks,), jnp.int32),
            smem((forks,), jnp.int32),
            smem((forks,), jnp.int32),
            dma((6,)),
            vmem(cache.shape, bf16),
            vmem((pairs, 2 * HEAD_DIM, slots), bf16),
            vmem((pairs, FRESH_ROWS, 2 * HEAD_DIM), bf16),
            vmem((pairs, FRESH_ROWS, 2 * HEAD_DIM), bf16),
            vmem((n, pairs, lanes, HEAD_DIM), bf16),
            vmem((n, pairs, HEAD_DIM, lanes), f32),
            vmem((n, pairs, 8, lanes), f32),
            vmem((n + 1, pairs, HEAD_DIM, lanes), i16),
            vmem((n + 1, pairs, 8, lanes), f32),
            vmem((n, pairs, HEAD_DIM, lanes), i16),
            vmem((n, pairs, 8, lanes), f32),
            vmem(parcel, bf16),
            vmem(parcel, bf16),
            dma((forks,)),
            dma((2, n, CHUNKS)),
            dma((n, CHUNKS)),
            dma((n, CHUNKS)),
            dma((n, CHUNKS)),
            dma((n + 1, CHUNKS)),
            dma((n + 1, CHUNKS)),
            dma((n,)),
            dma((n,)),
        ],
        compiler_params=pltpu.CompilerParams(
            collective_id=0, has_side_effects=True, vmem_limit_bytes=63 * 1024 * 1024
        ),
        cost_estimate=pl.CostEstimate(
            flops=work * 8 * HEAD_DIM, bytes_accessed=2 * cache.size, transcendentals=work
        ),
    )(queries, tool_key_value, cache, placed.reshape(-1), blocks.reshape(-1), span_len, owner)
    return pl.pallas_call(
        hand_over,
        out_shape=(
            jax.ShapeDtypeStruct(attended.shape, bf16),
            jax.ShapeDtypeStruct(owned.shape, bf16),
        ),
        in_specs=[pl.BlockSpec(memory_space=vmem)] * 2,
        out_specs=(pl.BlockSpec(memory_space=vmem),) * 2,
        compiler_params=pltpu.CompilerParams(vmem_limit_bytes=63 * 1024 * 1024),
    )(attended, owned)


def solution(mesh):
    return jax.shard_map(
        body,
        mesh=mesh,
        in_specs=(
            P(("groups", "rep"), "inst", "tp"),
            P(("groups", "rep"), "inst", "tp"),
            P(("groups", "rep"), "inst", "tp"),
            P(("groups", "rep"), "inst"),
            P(("groups", "rep"), "inst"),
            P(("groups", "rep")),
            P(("groups", "rep")),
        ),
        out_specs=(P(("groups", "rep"), "inst", "tp"), P(("groups", "inst"), "rep", None, "tp")),
        check_vma=False,
    )
```

```python
import functools
import math

import jax
import jax.numpy as jnp
from jax import lax
from jax.experimental import pallas as pl
from jax.experimental.pallas import tpu as pltpu
from jax.sharding import PartitionSpec as P

HEAD_DIM = 128
BLOCK = 128
FRESH_ROWS = 16
CHUNKS = 4
STEPS = 32000.0
LOG2E = 1.4426950408889634
HIDDEN = -1e30
FLOOR = -1e5
MESH = pl.DeviceIdType.MESH
NT = (((1,), (1,)), ((), ()))
TN = (((0,), (0,)), ((), ()))


def kernel(
    n, q_hbm, kv_hbm, cache_ref, placed_hbm, blocks_hbm, span_hbm, owner_hbm,
    att_ref, owned_ref,
    q_ref, kv_ref, placed_ref, blocks_ref, span_ref, owner_ref, input_sem,
    cbuf, vt, kf, vf, qbuf, pn, ps, ci, cis, co, cos, po, pi,
    cache_sem, q_send, q_recv, c_send, s_send, c_recv, s_recv, o_send, o_recv,
):
    forks, tokens, width = q_ref.shape
    width_kv = kv_ref.shape[2]
    kv_heads = width_kv // (2 * HEAD_DIM)
    group = width // (kv_heads * HEAD_DIM)
    rows = group * tokens
    lanes = 2 * rows
    pairs = forks * kv_heads // 2
    slots = cache_ref.shape[1]
    per = pairs // CHUNKS
    factor = LOG2E / math.sqrt(HEAD_DIM)
    me = lax.axis_index("inst")

    inputs = [
        pltpu.make_async_copy(source, target, input_sem.at[k])
        for k, (source, target) in enumerate(
            (
                (q_hbm, q_ref), (kv_hbm, kv_ref), (placed_hbm, placed_ref),
                (blocks_hbm, blocks_ref), (span_hbm, span_ref), (owner_hbm, owner_ref),
            )
        )
    ]
    for fetch in inputs:
        fetch.start()
    fetches = [
        pltpu.make_async_copy(cache_ref.at[f], cbuf.at[f], cache_sem.at[f])
        for f in range(forks)
    ]
    for fetch in fetches:
        fetch.start()

    barrier = pltpu.get_barrier_semaphore()
    for k in range(1, n):
        pl.semaphore_signal(
            barrier, inc=1, device_id={"inst": lax.rem(me + k, n)}, device_id_type=MESH
        )

    def members(p):
        return [(u // kv_heads, u % kv_heads) for u in (2 * p, 2 * p + 1)]

    inputs[0].wait()
    for p in range(pairs):
        parts = []
        for f, j in members(p):
            for g in range(group):
                at = (j * group + g) * HEAD_DIM
                parts.append(q_ref[f, :, at : at + HEAD_DIM].astype(jnp.float32))
        qbuf[me, p] = jnp.concatenate(parts, axis=0).astype(jnp.bfloat16)

    pl.semaphore_wait(barrier, n - 1)

    def q_copy(origin, c, side):
        part = qbuf.at[origin, pl.ds(c * per, per)]
        return pltpu.make_async_remote_copy(
            src_ref=part, dst_ref=part,
            send_sem=q_send.at[side, origin, c], recv_sem=q_recv.at[origin, c],
            device_id={"inst": me + 1 if side == 0 else me - 1}, device_id_type=MESH,
        )

    for c in range(CHUNKS):
        for side in range(2):
            @pl.when(me + 1 < n if side == 0 else me > 0)
            def _():
                q_copy(me, c, side).start()

    for fetch in inputs[1:]:
        fetch.wait()
    for i in range(n):
        chosen = None
        for f in range(forks):
            tile = kv_ref[f].astype(jnp.float32)
            token = me * tokens + lax.broadcasted_iota(jnp.int32, tile.shape, 0)
            keep = (token < span_ref[f]) & (jnp.broadcast_to(owner_ref[f], tile.shape) == i)
            tile = jnp.where(keep, tile, 0.0)
            chosen = tile if chosen is None else chosen + tile
        po[i] = jnp.concatenate(
            [chosen[:, a : a + HEAD_DIM] for a in range(0, width_kv, HEAD_DIM)], axis=0
        ).astype(jnp.bfloat16)
    pi[me] = po[me]

    def parcel(k):
        target = lax.rem(me + k, n)
        return pltpu.make_async_remote_copy(
            src_ref=po.at[target], dst_ref=pi.at[me],
            send_sem=o_send.at[target], recv_sem=o_recv.at[me],
            device_id={"inst": target}, device_id_type=MESH,
        )

    for p in range(pairs):
        for ref, shift in ((kf, 0), (vf, HEAD_DIM)):
            both = [
                kv_ref[f, :, 2 * j * HEAD_DIM + shift : 2 * j * HEAD_DIM + shift + HEAD_DIM]
                for f, j in members(p)
            ]
            tile = jnp.concatenate(both, axis=1).astype(jnp.float32)
            pad = jnp.zeros((FRESH_ROWS - tokens, 2 * HEAD_DIM), jnp.float32)
            ref[p] = jnp.concatenate([tile, pad], axis=0).astype(jnp.bfloat16)

    for fetch in fetches:
        fetch.wait()
    for p in range(pairs):
        for h, (f, j) in enumerate(members(p)):
            at = (2 * j + 1) * HEAD_DIM
            vt[p, h * HEAD_DIM : (h + 1) * HEAD_DIM, :] = cbuf[f, :, at : at + HEAD_DIM].T

    lane = lax.broadcasted_iota(jnp.int32, (1, lanes), 1)
    lane_token = lax.rem(lane, tokens)
    first = lane < rows

    def by_lane(p, value):
        (f0, _), (f1, _) = members(p)
        return jnp.where(first, value(f0), value(f1))

    def spread(origin, p):
        tile = qbuf[origin, p]
        blank = jnp.zeros((rows, HEAD_DIM), jnp.bfloat16)
        return jnp.concatenate(
            [
                jnp.concatenate([tile[:rows], blank], axis=1),
                jnp.concatenate([blank, tile[rows:]], axis=1),
            ],
            axis=0,
        )

    def scores(origins, p):
        against = jnp.concatenate([spread(origin, p) for origin in origins], axis=0)
        keys = jnp.concatenate(
            [cbuf[f, :, 2 * j * HEAD_DIM : (2 * j + 1) * HEAD_DIM] for f, j in members(p)], axis=1
        )
        score = lax.dot_general(keys, against, NT, preferred_element_type=jnp.float32)
        score_new = lax.dot_general(kf[p], against, NT, preferred_element_type=jnp.float32)
        return score, score_new

    def weigh(origin, p, score, score_new):
        live = by_lane(p, lambda f: placed_ref[f] * blocks_ref[f])
        tiles = [score[a : a + BLOCK].reshape(-1, 8, lanes) for a in range(0, slots, BLOCK)]
        row = lax.broadcasted_iota(jnp.int32, (FRESH_ROWS, lanes), 0)
        counted = (row < tokens) & (me * tokens + row <= origin * tokens + lane_token)
        score_new = jnp.where(counted, score_new * factor, HIDDEN)
        top = jnp.max(score_new.reshape(-1, 8, lanes), axis=0)
        for b, tile in enumerate(tiles):
            top = jnp.maximum(top, jnp.where(b < live, jnp.max(tile, axis=0) * factor, HIDDEN))
        top = jnp.maximum(jnp.max(top, axis=0, keepdims=True), FLOOR)
        weight_new = jnp.exp2(score_new - top)
        total = jnp.sum(weight_new.reshape(-1, 8, lanes), axis=0)
        weights = []
        for b, tile in enumerate(tiles):
            shift = jnp.where(b < live, top, -HIDDEN)
            weight = jnp.exp2(tile * factor - shift[None])
            total = total + jnp.sum(weight, axis=0)
            weights.append(weight.reshape(BLOCK, lanes).astype(jnp.bfloat16))
        total = jnp.sum(total, axis=0, keepdims=True)
        return jnp.concatenate(weights, axis=0), weight_new.astype(jnp.bfloat16), top, total

    def partials(origins, p, score, score_new):
        parts = [
            weigh(
                origin, p, score[:, k * lanes : (k + 1) * lanes],
                score_new[:, k * lanes : (k + 1) * lanes],
            )
            for k, origin in enumerate(origins)
        ]
        weight = jnp.concatenate([part[0] for part in parts], axis=1)
        weight_new = jnp.concatenate([part[1] for part in parts], axis=1)
        both = jnp.dot(vt[p], weight, preferred_element_type=jnp.float32)
        both = both + lax.dot_general(vf[p], weight_new, TN, preferred_element_type=jnp.float32)
        return [
            (
                jnp.where(
                    first,
                    both[:HEAD_DIM, k * lanes : (k + 1) * lanes],
                    both[HEAD_DIM:, k * lanes : (k + 1) * lanes],
                ),
                part[2],
                part[3],
            )
            for k, part in enumerate(parts)
        ]

    def attend(origins, after=None):
        ahead = scores(origins, 0)
        for p in range(pairs):
            now = ahead
            if p + 1 < pairs:
                ahead = scores(origins, p + 1)
            for origin, part in zip(origins, partials(origins, p, *now)):
                pn[origin, p], ps[origin, p, 0:1], ps[origin, p, 1:2] = part
            if after is not None:
                after(p)

    def kept(d, p):
        return pn[d, p], ps[d, p, 0:1], ps[d, p, 1:2]

    def arrived(slot, p):
        numer = ci[slot, p].astype(jnp.int32).astype(jnp.float32) * cis[slot, p, 2:3]
        return numer, cis[slot, p, 0:1], cis[slot, p, 1:2]

    def merge(one, two):
        top = jnp.maximum(one[1], two[1])
        a = jnp.exp2(one[1] - top)
        b = jnp.exp2(two[1] - top)
        return a * one[0] + b * two[0], top, a * one[2] + b * two[2]

    def pack(d, p, part):
        numer, top, total = part
        reach = jnp.maximum(jnp.max(jnp.abs(numer), axis=0, keepdims=True), 1e-30)
        co[d, p] = jnp.round(numer * (STEPS / reach)).astype(jnp.int32).astype(jnp.int16)
        row = lax.broadcasted_iota(jnp.int32, (8, lanes), 0)
        cos[d, p] = jnp.where(row == 0, top, jnp.where(row == 1, total, reach * (1.0 / STEPS)))

    def chain_copies(d, c, side):
        target = me + 1 - 2 * side
        slot = jnp.where((d == target) & (side == 1), n, d)
        part = pl.ds(c * per, per)
        where = dict(device_id={"inst": target}, device_id_type=MESH)
        return (
            pltpu.make_async_remote_copy(
                src_ref=co.at[d, part], dst_ref=ci.at[slot, part],
                send_sem=c_send.at[d, c], recv_sem=c_recv.at[slot, c], **where
            ),
            pltpu.make_async_remote_copy(
                src_ref=cos.at[d, part], dst_ref=cis.at[slot, part],
                send_sem=s_send.at[d, c], recv_sem=s_recv.at[slot, c], **where
            ),
        )

    def chain_arrival(slot, c):
        part = pl.ds(c * per, per)
        pltpu.make_async_copy(ci.at[slot, part], ci.at[slot, part], c_recv.at[slot, c]).wait()
        pltpu.make_async_copy(cis.at[slot, part], cis.at[slot, part], s_recv.at[slot, c]).wait()

    at_end = (me == 0) | (me == n - 1)
    end_side = jnp.where(me == 0, 0, 1)

    def relay(t, chunks):
        for side in range(2):
            origin = me - t if side == 0 else me + t
            there = origin >= 0 if side == 0 else origin < n
            onward = me + 1 < n if side == 0 else me > 0

            @pl.when(there & onward)
            def _():
                for c in chunks:
                    q_copy(origin, c, side).wait_recv()
                    q_copy(origin, c, side).start()

    def relay_part(t, parts):
        size = -(-CHUNKS // parts)
        return lambda p: relay(
            t, range(min(1 + p * size, CHUNKS), min(1 + (p + 1) * size, CHUNKS))
        )

    def chain_step(d, c, side):
        chain_arrival(d, c)
        for p in range(c * per, (c + 1) * per):
            pack(d, p, merge(kept(d, p), arrived(d, p)))
        for copy in chain_copies(d, c, side):
            copy.start()

    relay(1, range(1))
    attend([me], relay_part(1, pairs))

    def advance(t, carry):
        @pl.when(t == n // 2)
        def _():
            for k in range(1, n):
                parcel(k).start()

        @pl.when(at_end & (t < n))
        def _():
            origin = me + t * (1 - 2 * end_side)

            def arrive(c):
                q_copy(origin, c, 0).wait_recv()
                return [(p, scores([origin], p)) for p in range(c * per, (c + 1) * per)]

            ahead = arrive(0)
            for c in range(CHUNKS):
                now = ahead
                if c + 1 < CHUNKS:
                    ahead = arrive(c + 1)
                for p, score in now:
                    pack(origin, p, partials([origin], p, *score)[0])
                for copy in chain_copies(origin, c, end_side):
                    copy.start()

        @pl.when(jnp.logical_not(at_end))
        def _():
            before, beyond = me - t >= 0, me + t < n

            @pl.when(before & beyond)
            def _():
                relay(t + 1, range(1))
                attend([me - t, me + t], relay_part(t + 1, pairs // 2))

            @pl.when(jnp.logical_not(before & beyond))
            def _():
                @pl.when(before | beyond)
                def _():
                    attend([jnp.where(before, me - t, me + t)])

                relay(t + 1, range(CHUNKS))

            for side in range(2):
                place = me if side == 0 else n - 1 - me
                far = t - place
                d = far if side == 0 else n - 1 - far


                @pl.when((far > place) & (far < n))
                def _():
                    for c in range(CHUNKS):
                        chain_step(d, c, side)

        return carry

    lax.fori_loop(1, 2 * n - 1, advance, 0)

    for k in range(1, n):
        source = lax.rem(me + n - k, n)
        pltpu.make_async_copy(pi.at[source], pi.at[source], o_recv.at[source]).wait()
    gathered = [pi[i].astype(jnp.float32) for i in range(n)]
    for a in range(width_kv // HEAD_DIM):
        column = jnp.concatenate([x[a * tokens : (a + 1) * tokens] for x in gathered], axis=0)
        owned_ref[0, 0, :, a * HEAD_DIM : (a + 1) * HEAD_DIM] = column.astype(jnp.bfloat16)

    for c in range(CHUNKS):
        for slot, there in ((me, me > 0), (n, me + 1 < n)):
            @pl.when(there)
            def _():
                chain_arrival(slot, c)
                for p in range(c * per, (c + 1) * per):
                    numer, top, total = merge(kept(me, p), arrived(slot, p))
                    pn[me, p] = numer
                    ps[me, p, 0:1] = top
                    ps[me, p, 1:2] = total

        for p in range(c * per, (c + 1) * per):
            numer, _, total = kept(me, p)
            span = by_lane(p, lambda f: span_ref[f])
            result = jnp.where(me * tokens + lane_token < span, numer / total, 0.0).T
            for h, (f, j) in enumerate(members(p)):
                for g in range(group):
                    at = (j * group + g) * HEAD_DIM
                    start = h * rows + g * tokens
                    att_ref[f, :, at : at + HEAD_DIM] = result[start : start + tokens].astype(
                        jnp.bfloat16
                    )

    for k in range(1, n):
        parcel(k).wait_send()
    for c in range(CHUNKS):
        for side in range(2):
            @pl.when(me + 1 < n if side == 0 else me > 0)
            def _():
                q_copy(me, c, side).wait_send()

    def drain(t, carry):
        for c in range(CHUNKS):
            for side in range(2):
                origin = me - t if side == 0 else me + t
                onward = me + 1 < n if side == 0 else me > 0

                @pl.when((origin >= 0 if side == 0 else origin < n) & onward)
                def _():
                    q_copy(origin, c, side).wait_send()

                d = me + t if side == 0 else me - t

                @pl.when(d < n if side == 0 else d >= 0)
                def _():
                    for copy in chain_copies(d, c, side):
                        copy.wait_send()
        return carry

    lax.fori_loop(1, n, drain, 0)


def hand_over(attended, owned, attended_out, owned_out):
    attended_out[...] = attended[...]
    owned_out[...] = owned[...]


def body(queries, tool_key_value, cache, placed, blocks, span_len, owner):
    n = lax.axis_size("inst")
    forks, tokens, width = queries.shape
    width_kv = tool_key_value.shape[2]
    slots = cache.shape[1]
    kv_heads = width_kv // (2 * HEAD_DIM)
    group = width // (kv_heads * HEAD_DIM)
    pairs = forks * kv_heads // 2
    lanes = 2 * group * tokens
    parcel = (n, tokens * width_kv // HEAD_DIM, HEAD_DIM)
    bf16, f32, i16 = jnp.bfloat16, jnp.float32, jnp.int16
    vmem, smem = pltpu.VMEM, pltpu.SMEM
    dma = pltpu.SemaphoreType.DMA
    work = n * pairs * slots * lanes
    attended, owned = pl.pallas_call(
        functools.partial(kernel, n),
        out_shape=(
            jax.ShapeDtypeStruct(queries.shape, bf16),
            jax.ShapeDtypeStruct((1, 1, n * tokens, width_kv), bf16),
        ),
        in_specs=[
            pl.BlockSpec(memory_space=pltpu.HBM)
        ]
        * 7,
        out_specs=(pl.BlockSpec(memory_space=vmem), pl.BlockSpec(memory_space=vmem)),
        scratch_shapes=[
            vmem(queries.shape, bf16),
            vmem(tool_key_value.shape, bf16),
            smem((forks,), jnp.int32),
            smem((forks,), jnp.int32),
            smem((forks,), jnp.int32),
            smem((forks,), jnp.int32),
            dma((6,)),
            vmem(cache.shape, bf16),
            vmem((pairs, 2 * HEAD_DIM, slots), bf16),
            vmem((pairs, FRESH_ROWS, 2 * HEAD_DIM), bf16),
            vmem((pairs, FRESH_ROWS, 2 * HEAD_DIM), bf16),
            vmem((n, pairs, lanes, HEAD_DIM), bf16),
            vmem((n, pairs, HEAD_DIM, lanes), f32),
            vmem((n, pairs, 8, lanes), f32),
            vmem((n + 1, pairs, HEAD_DIM, lanes), i16),
            vmem((n + 1, pairs, 8, lanes), f32),
            vmem((n, pairs, HEAD_DIM, lanes), i16),
            vmem((n, pairs, 8, lanes), f32),
            vmem(parcel, bf16),
            vmem(parcel, bf16),
            dma((forks,)),
            dma((2, n, CHUNKS)),
            dma((n, CHUNKS)),
            dma((n, CHUNKS)),
            dma((n, CHUNKS)),
            dma((n + 1, CHUNKS)),
            dma((n + 1, CHUNKS)),
            dma((n,)),
            dma((n,)),
        ],
        compiler_params=pltpu.CompilerParams(
            collective_id=0, has_side_effects=True, vmem_limit_bytes=63 * 1024 * 1024
        ),
        cost_estimate=pl.CostEstimate(
            flops=work * 8 * HEAD_DIM, bytes_accessed=2 * cache.size, transcendentals=work
        ),
    )(queries, tool_key_value, cache, placed.reshape(-1), blocks.reshape(-1), span_len, owner)
    return pl.pallas_call(
        hand_over,
        out_shape=(
            jax.ShapeDtypeStruct(attended.shape, bf16),
            jax.ShapeDtypeStruct(owned.shape, bf16),
        ),
        in_specs=[pl.BlockSpec(memory_space=vmem)] * 2,
        out_specs=(pl.BlockSpec(memory_space=vmem),) * 2,
        compiler_params=pltpu.CompilerParams(vmem_limit_bytes=63 * 1024 * 1024),
    )(attended, owned)


def solution(mesh):
    return jax.shard_map(
        body,
        mesh=mesh,
        in_specs=(
            P(("groups", "rep"), "inst", "tp"),
            P(("groups", "rep"), "inst", "tp"),
            P(("groups", "rep"), "inst", "tp"),
            P(("groups", "rep"), "inst"),
            P(("groups", "rep"), "inst"),
            P(("groups", "rep")),
            P(("groups", "rep")),
        ),
        out_specs=(P(("groups", "rep"), "inst", "tp"), P(("groups", "inst"), "rep", None, "tp")),
        check_vma=False,
    )
```
